1024 devices in a mesh: dp: 8 (over z_hi, y), expert: 64 (over x, z_lo), tensor: 2 (over core).
Axes of the slice: x: 4, y: 4, z: 32 (z_hi: 2, z_lo: 16; z = z_hi * 16 + z_lo), core: 2. Of those that a mesh axis runs over, the one named last changes fastest.
Arguments:
- layer_input: bfloat16 [8192, 7168], P('expert'), may hold values from -0.875 to 0.875
- routes: int32 [8192, 2], P('expert'), may hold values from 0 to 31, all different within a row; in each aligned block of 128 rows (0 to 127, 128 to 255, ...) at most 12 rows name the same one
- dense_cot: bfloat16 [8192, 2560], P('expert', ('dp', 'tensor')), may hold values from -1.5 to 1.5
- dense_weight: bfloat16 [7168, 2560], P(None, ('dp', 'tensor')), may hold values from -0.125 to 0.125
- expert_cot: bfloat16 [768, 81920], P(None, 'expert'), may hold values from -6 to 6
- expert_weight: bfloat16 [7168, 81920], P(('dp', 'tensor'), 'expert'), may hold values from -0.125 to 0.125
Outputs:
- input_grad: bfloat16 [8192, 7168], P('expert', ('dp', 'tensor'))
- dense_wgrad: float32 [7168, 2560], P('expert', ('dp', 'tensor'))
- expert_wgrad: bfloat16 [7168, 81920], P(('dp', 'tensor'), 'expert')
The draws below stay inside these ranges and needn't reach their ends.
Inputs may be any that keep to these rules, and one draw needn't show every extreme that they name: `routes`: the two experts of a token differ. Among the 128 tokens of one device no expert is named more than 12 times, and in every draw some device names some expert exactly 12 times.
All inputs are finite; a program needn't handle non-finite values.
Results may differ from the reference program's by a relative error of at most 0.0065.
Values may be sent and summed in bfloat16 or wider, within the bound.
A program may use at most 64 MiB of HBM per device.

```python
import math
import jax
import jax.numpy as jnp
import numpy as np
from jax import lax

D = 7168
HD = 2560
EH = 2560
TOK_DEV = 128
EXPERTS = 32
CAP = 12
TOKENS = 8192
N_DP = 8
N_EXPERT = 64
N_TENSOR = 2


def with_spikes(drawn, stream_key, source, target, shards_of, factor):
    owner, partner = [(jnp.arange(drawn.shape[axis_at]) // (drawn.shape[axis_at] // shards_of)).reshape([-1 if axis == axis_at else 1 for axis in range(drawn.ndim)]) for axis_at in (source, target)]
    chosen = jax.random.permutation(stream_key, shards_of)[partner]
    strong = (owner == chosen) | (owner == (partner + shards_of // 2) % shards_of)
    return jnp.where(strong, factor * drawn, drawn)


def shard_levels(rng, extent, cuts, least, top_value):
    level, own = 1.0, jax.random.fold_in(rng, 6)
    for dim, blocks in cuts:
        steps = jnp.exp(jax.random.uniform(jax.random.fold_in(own, dim), (blocks,), jnp.float32, least / len(cuts), top_value / len(cuts)))
        level = level * jnp.repeat(steps, extent[dim] // blocks).reshape([-1 if axis == dim else 1 for axis in range(len(extent))])
    return level


def shared_out(stream_key, own, number, rows, number_of, top, most, lean):
    sequence = jax.random.permutation(stream_key, number_of)
    crowded, ordinary = shares(number_of, rows * top, most, lean, True), shares(number_of, rows * top, most, lean, False)
    places = jnp.arange(number_of)

    def named(sizes, offset_by):
        used = int((sizes > 0).sum())
        fixed = max(1, used // 4)
        shifted = fixed + (places - fixed + offset_by * (used - fixed)) % max(1, number_of - fixed)
        return jnp.zeros((number_of,), jnp.int32).at[sequence[jnp.where(places < fixed, places, shifted)]].set(jnp.asarray(sizes, jnp.int32))

    sizes = jnp.where(number % 4 == 0, named(crowded, number // 4), named(ordinary, number - number // 4 - 1))
    mixed = jax.random.permutation(jax.random.fold_in(own, 3), number_of)
    giver, receiver = mixed[0:number_of // 2 * 2:2], mixed[1:number_of // 2 * 2:2]
    margin = jnp.minimum(sizes[giver] - 1, most - sizes[receiver]) // 2
    margin = jnp.where((giver == sequence[0]) | (receiver == sequence[0]) | (sizes[receiver] == 0), 0, jnp.maximum(margin, 0))
    shifted = jax.random.randint(jax.random.fold_in(own, 4), (number_of // 2,), 0, 1 << 20) % (margin + 1)
    sizes = sizes.at[giver].add(-shifted).at[receiver].add(shifted)
    items = jnp.searchsorted(jnp.cumsum(sizes), jnp.arange(rows * top), side="right").astype(jnp.int32)
    listing = items.reshape(top, rows).T
    listing = listing[jax.random.permutation(jax.random.fold_in(own, 1), rows)]
    offset_by = jax.random.randint(jax.random.fold_in(own, 2), (rows, 1), 0, top)
    return jnp.take_along_axis(listing, (jnp.arange(top)[None, :] + offset_by) % top, axis=1)


def shares(count, total, most, skew, full):
    loads = [(1 << 20) // math.isqrt(grade ** skew) + 1 for grade in range(1, count + 1)]
    largest = most if full else min(most, max(-(-total // count), total * loads[0] // sum(loads)))
    least = 1 if total - largest >= count - 1 else 0
    counts, surplus = [largest] + [least] * (count - 1), total - largest - least * (count - 1)
    while surplus > 0:
        candidates = [i for i in range(1, count) if counts[i] < largest] or [i for i in range(1, count) if counts[i] < most]
        whole, budget = sum([loads[i] for i in candidates]), surplus
        for i in candidates:
            more = min(most - counts[i], max(1, budget * loads[i] // whole), surplus)
            counts[i] = counts[i] + more
            surplus = surplus - more
    return np.array(counts)


def centred(own_key, extent, width, reach, split=(), kind=jnp.bfloat16):
    entries = jax.random.normal(own_key, extent, jnp.float32) * width
    if len(split) > 0:
        entries = shard_levels(own_key, extent, split, -0.22, 0.18) * entries
    return jnp.clip(entries, min=-reach, max=reach).astype(kind)


def heavy_noise(own_key, dims, scale, bound, shards, heavy, held_as=jnp.bfloat16):
    result = scale * jax.random.normal(own_key, dims, jnp.float32)
    if shards:
        result = result * shard_levels(own_key, dims, shards, -0.22, 0.18)
    return jnp.clip(with_spikes(result, jax.random.fold_in(own_key, 3), *heavy), -bound, bound).astype(held_as)


def setup_inputs(seed: int = 0) -> dict:
    streams_of = jax.random.split(jax.random.key(seed), 7)
    layer_input = heavy_noise(streams_of[0], (TOKENS, D), 0.05, 0.875, ((0, 64),), (0, 1, 64, 4.0))
    routes_keys = jax.random.split(jax.random.fold_in(streams_of[1], 1), TOKENS // TOK_DEV)
    routes_turns = jax.random.permutation(jax.random.fold_in(streams_of[1], 3), TOKENS // TOK_DEV)
    routes = jax.vmap(lambda own, number: shared_out(jax.random.fold_in(streams_of[1], 2), own, number, TOK_DEV, EXPERTS, 2, CAP, 2))(routes_keys, routes_turns).reshape((TOKENS, 2))
    dense_cot = centred(streams_of[2], (TOKENS, HD), 0.25, 1.5, ((0, 64), (1, 16)))
    dense_weight = centred(streams_of[3], (D, HD), HD ** -0.5, 0.125, ((1, 16),))
    expert_cot = centred(streams_of[4], (N_EXPERT * CAP, EXPERTS * EH), 1.0, 6.0, ((1, 64),))
    expert_weight = centred(streams_of[5], (D, EXPERTS * EH), EH ** -0.5, 0.125, ((0, 16), (1, 64)))
    return dict(layer_input=layer_input, routes=routes, dense_cot=dense_cot, dense_weight=dense_weight, expert_cot=expert_cot, expert_weight=expert_weight)


def slot_targets(routes):
    block_routes = routes.reshape(N_EXPERT, TOK_DEV * 2)
    onehot = (block_routes[:, :, None] == jnp.arange(EXPERTS, dtype=jnp.int32)[None, None, :]).astype(jnp.int32)
    earlier = jnp.cumsum(onehot, axis=1) - onehot
    slot_rank = jnp.sum(earlier * onehot, axis=2)
    source = jnp.arange(N_EXPERT, dtype=jnp.int32)[:, None]
    return (source * CAP + slot_rank).reshape(TOKENS, 2).astype(jnp.int32)


def reference(layer_input, routes, dense_cot, dense_weight, expert_cot, expert_weight):
    group_total = N_DP * N_TENSOR
    slice_width = HD // group_total
    dense_sum = jnp.zeros((TOKENS, D), jnp.float32)
    for group_id in range(group_total):
        first_col = group_id * slice_width
        partial_dense = jnp.dot(dense_cot[:, first_col:first_col + slice_width],
                                dense_weight[:, first_col:first_col + slice_width].T,
                                preferred_element_type=jnp.float32)
        rounded = lax.optimization_barrier(partial_dense.astype(jnp.bfloat16))
        dense_sum = dense_sum + rounded.astype(jnp.float32)
    dense_wgrad = jnp.dot(layer_input.T, dense_cot, preferred_element_type=jnp.float32)
    targets = slot_targets(routes)
    slot_total = N_EXPERT * CAP
    repeated = jnp.repeat(layer_input, 2, axis=0)
    half_width = EH // 2

    def per_expert(carry, expert_id):
        chosen = routes == expert_id
        where_slot = jnp.where(chosen, targets, slot_total).reshape(-1).astype(jnp.int32)
        gathered = jnp.zeros((slot_total + 1, D), layer_input.dtype).at[where_slot].set(repeated)[:slot_total]
        cot_block = lax.dynamic_slice_in_dim(expert_cot, (expert_id * EH).astype(jnp.int32), EH, 1)
        weight_block = lax.dynamic_slice_in_dim(expert_weight, (expert_id * EH).astype(jnp.int32), EH, 1)
        grad_block = jnp.dot(gathered.T, cot_block, preferred_element_type=jnp.float32).astype(jnp.bfloat16)
        lower = jnp.dot(cot_block[:, :half_width], weight_block[:, :half_width].T, preferred_element_type=jnp.float32)
        upper = jnp.dot(cot_block[:, half_width:], weight_block[:, half_width:].T, preferred_element_type=jnp.float32)
        lower_rounded = lax.optimization_barrier(lower.astype(jnp.bfloat16))
        upper_rounded = lax.optimization_barrier(upper.astype(jnp.bfloat16))
        pieces = lower_rounded.astype(jnp.float32) + upper_rounded.astype(jnp.float32)
        safe_slot = jnp.where(chosen, targets, 0).astype(jnp.int32)
        updated = carry
        for column in range(2):
            picked = pieces[safe_slot[:, column]]
            updated = updated + jnp.where(chosen[:, column][:, None], picked, jnp.zeros_like(picked))
        return updated, grad_block

    expert_sum, grads = lax.scan(per_expert, jnp.zeros((TOKENS, D), jnp.float32),
                                 jnp.arange(EXPERTS, dtype=jnp.int32))
    expert_wgrad = grads.transpose(1, 0, 2).reshape(D, EXPERTS * EH)
    input_grad = (dense_sum + expert_sum).astype(jnp.bfloat16)
    return (input_grad, dense_wgrad, expert_wgrad)
```

```python
import functools

import jax
import jax.numpy as jnp
import numpy as np
from jax import lax
from jax.experimental import pallas as pl
from jax.experimental.pallas import tpu as pltpu
from jax.sharding import PartitionSpec as P

MESH = pl.DeviceIdType.MESH
F32 = jnp.float32
BF16 = jnp.bfloat16
CAP = 12
NX, NY = 4, 4


def dot(a, b, ca, cb):
    return lax.dot_general(a, b, (((ca,), (cb,)), ((), ())), preferred_element_type=F32)


def rev_bits(q, bits):
    return sum(((q >> b) & 1) << (bits - 1 - b) for b in range(bits))


def up(n, m):
    return -(-n // m) * m


def kernel(
    dims,
    li, rt, cot, wt, ecot, ew, p_x, p_z, e_mat, m_mat,
    o_in, o_dw, o_ew,
    dmat, xs, xr, zs, zr, prt, pz, pin, rs, rz, qs, rx,
    dacc, dsend, dcore, ysend, yrecv, hsend, hrecv,
    wxs, wxr, wz, wzr,
    dx_s, dx_r, dz_s, dz_r, df_s, df_r, pe_s, pe_r, rz_s, rz_r, rx_s, rx_r,
    c_s, c_r, y_s, y_r, h_s, h_r, wx_s, wx_r, wz_s, wz_r,
):
    nx, nz, ny, nh = dims
    pairs = nz // 2
    bits = nz.bit_length() - 1
    feat = ew.shape[0]
    fpad = xs.shape[2]
    wl = o_dw.shape[1]
    win_w = nz * wl
    rowx = pairs * CAP
    dp = lax.axis_index("dp")
    ex = lax.axis_index("expert")
    core = lax.axis_index("tensor")
    x, z = ex // nz, ex % nz
    zh, y = dp // ny, dp % ny
    pair, par = z // 2, z % 2

    def at_x(d):
        return (dp, lax.rem(x + d, nx) * nz + z, core)

    def at_z(zz):
        return (dp, x * nz + zz, core)

    def at_pair(d):
        return at_z(lax.rem(pair + d, pairs) * 2 + par)

    beside = at_z(z + 1 - 2 * par)
    other_core = (dp, ex, 1 - core)

    def at_y(d):
        return (zh * ny + lax.rem(y + d, ny), ex, core)

    other_h = ((1 - zh) * ny + y, ex, core)

    def copy(src, dst, send, recv, dev):
        return pltpu.make_async_remote_copy(
            src_ref=src, dst_ref=dst, send_sem=send, recv_sem=recv,
            device_id=dev, device_id_type=MESH,
        )

    met = [at_x(d) for d in range(1, nx)] + [at_pair(d) for d in range(1, pairs)]
    met += [beside, other_core] + [at_y(d) for d in range(1, ny)] + [other_h]
    barrier = pltpu.get_barrier_semaphore()
    for dev in met:
        pl.semaphore_signal(barrier, inc=1, device_id=dev, device_id_type=MESH)

    r = rt[...]
    e_row = lax.broadcasted_iota(jnp.int32, (e_mat.shape[1], r.shape[1]), 0)
    member = ((e_row == r[0:1, :]) | (e_row == r[1:2, :])).astype(F32).astype(BF16)
    n_tok = r.shape[1]
    before = lax.broadcasted_iota(jnp.int32, (n_tok, n_tok), 0) < lax.broadcasted_iota(
        jnp.int32, (n_tok, n_tok), 1
    )
    rank = dot(member, before.astype(F32).astype(BF16), 1, 0).astype(BF16)
    is_member = dot(e_mat[...], member, 1, 0)
    ranks = dot(e_mat[...], rank, 1, 0)
    dmat[...] = ((is_member > 0.5) & (ranks == m_mat[...])).astype(F32).astype(BF16)
    chip_w = 2 * feat
    window = li[:, pl.ds(pl.multiple_of(dp * chip_w, 128), chip_w)]
    pick_r = lax.broadcasted_iota(jnp.int32, (chip_w, fpad), 0)
    pick_c = lax.broadcasted_iota(jnp.int32, (chip_w, fpad), 1)
    pick = ((pick_r == pick_c + core * feat) & (pick_c < feat)).astype(F32).astype(BF16)
    mine = dot(window, pick, 1, 0).astype(BF16)
    for i in range(nx):
        xs[i] = dot(dmat[i * rowx:(i + 1) * rowx, :], mine, 1, 0).astype(BF16)
    xr[x] = xs[x]

    pl.semaphore_wait(barrier, len(met))

    def dx_copy(d, slot):
        return copy(xs.at[lax.rem(x + d, nx)], xr.at[slot], dx_s.at[d], dx_r.at[d], at_x(d))

    for d in range(1, nx):
        dx_copy(d, x).start()

    rows_t = ecot.shape[0] // 4
    @pl.loop(0, 4)
    def _(i):
        at = pl.ds(pl.multiple_of(i * rows_t, 16), rows_t)
        prt[at, :] = dot(ecot[at, :], ew[...], 1, 1).astype(BF16)

    blk = nx * CAP
    pz[:, :, :, feat:] = jnp.zeros((2, pairs, blk, fpad - feat), BF16)
    for i in range(2):
        half = p_z[i * pairs * blk:(i + 1) * pairs * blk, :]
        pz[i, :, :, 0:feat] = dot(half, prt[...], 1, 0).astype(BF16).reshape(pairs, blk, feat)

    def pe_copy(k):
        return copy(pz.at[1 - par, k], pin.at[k], pe_s.at[k], pe_r.at[k], beside)

    @pl.loop(0, pairs)
    def _(k):
        pe_copy(k).start()

    def wx_copy(d):
        return copy(wxs.at[d - 1], wxr.at[d - 1], wx_s.at[d], wx_r.at[d], at_x(d))

    def wblock(xx):
        w_in = li[:, pl.ds(pl.multiple_of(xx * win_w, 128), win_w)]
        return dot(cot[...], w_in, 1, 0)

    for d in range(1, nx):
        got = wblock(lax.rem(x + d, nx))
        for q in range(nz):
            wxs[d - 1, rev_bits(q, bits), :, 0:wl] = got[:, q * wl:(q + 1) * wl].astype(BF16)
        wxs[d - 1, :, :, wl:] = jnp.zeros((nz, wxs.shape[2], wxs.shape[3] - wl), BF16)
        wx_copy(d).start()
    got = wblock(x)
    for q in range(nz):
        wz[rev_bits(q, bits), :, 0:wl] = got[:, q * wl:(q + 1) * wl]
    wz[:, :, wl:] = jnp.zeros((nz, wz.shape[1], wz.shape[2] - wl), F32)

    for d in range(1, nx):
        dx_copy(d, lax.rem(x + nx - d, nx)).wait_recv()
    zs[...] = dot(p_x[...], xr[...].reshape(nx * rowx, fpad), 1, 0).astype(BF16).reshape(
        pairs, blk, fpad
    )

    def dz_copy(d, slot):
        return copy(
            zs.at[lax.rem(pair + d, pairs)], zr.at[par, slot], dz_s.at[d], dz_r.at[d], at_pair(d)
        )

    def df_copy(d, side):
        slot = lax.rem(pair + pairs - d, pairs)
        return copy(zr.at[side, slot], zr.at[side, slot], df_s.at[d], df_r.at[d], beside)

    @pl.loop(1, pairs)
    def _(d):
        dz_copy(d, pair).start()

    zr[par, pair] = zs[pair]
    df_copy(0, par).start()

    def rz_copy(d, slot):
        return copy(
            rs.at[lax.rem(pair + d, pairs)], rz.at[slot], rz_s.at[d], rz_r.at[d], at_pair(d)
        )

    @pl.loop(1, pairs)
    def _(d):
        k = lax.rem(pair + d, pairs)
        pe_copy(k).wait_recv()
        rs[k] = (pz[par, k].astype(F32) + pin[k].astype(F32)).astype(BF16)
        rz_copy(d, pair).start()

    pe_copy(pair).wait_recv()
    rz[pair] = (pz[par, pair].astype(F32) + pin[pair].astype(F32)).astype(BF16)

    def c_copy(k):
        return copy(dsend.at[k], dcore.at[k], c_s.at[k], c_r.at[k], other_core)

    @pl.loop(0, nh * ny)
    def _(k):
        part = dot(wt[:, pl.ds(pl.multiple_of(k * chip_w, 128), chip_w)], cot[...], 0, 0)
        low, high = part[0:feat, :], part[feat:, :]
        dacc[k] = jnp.where(core == 0, low, high)
        dsend[k] = jnp.where(core == 0, high, low).astype(BF16)
        c_copy(k).start()

    def y_copy(d):
        return copy(ysend.at[d - 1], yrecv.at[d - 1], y_s.at[d], y_r.at[d], at_y(d))

    def core_sum(k):
        c_copy(k).wait_recv()
        return dacc[k] + dcore[k].astype(F32)

    for d in range(1, ny):
        for h in range(nh):
            ysend[d - 1, h] = core_sum(h * ny + lax.rem(y + d, ny)).astype(BF16)
        y_copy(d).start()
    for h in range(nh):
        dacc[h * ny + y] = core_sum(h * ny + y)

    for d in range(1, nx):
        wx_copy(d).wait_recv()

    @pl.loop(0, nz)
    def _(i):
        total = wz[i]
        for d in range(1, nx):
            total = total + wxr[d - 1, i].astype(F32)
        wz[i] = total

    def wz_at(step):
        base, size = 0, nz
        for b in range(step):
            size = size // 2
            base = base + ((z // (1 << b)) % 2) * size
        return base, size

    def wz_copy(step):
        base, size = wz_at(step)
        size = size // 2
        bit = (z // (1 << step)) % 2
        away = base + (1 - bit) * size
        land = nz - 2 * size
        partner = at_z(z + (1 - 2 * bit) * (1 << step))
        return copy(
            wz.at[pl.ds(away, size)], wzr.at[pl.ds(land, size)],
            wz_s.at[step], wz_r.at[step], partner,
        )

    def wz_add(step):
        wz_copy(step).wait_recv()
        base, size = wz_at(step + 1)
        land = nz - 2 * size

        @pl.loop(0, size)
        def _(i):
            wz[base + i] = wz[base + i] + wzr[land + i]

    wz_copy(0).start()

    @pl.loop(1, pairs)
    def _(d):
        dz_copy(d, lax.rem(pair + pairs - d, pairs)).wait_recv()
        df_copy(d, par).start()

    def h_copy():
        return copy(hsend, hrecv, h_s.at[0], h_r.at[0], other_h)

    for d in range(1, ny):
        y_copy(d).wait_recv()
    for h in range(nh):
        total = dacc[h * ny + y]
        for d in range(1, ny):
            total = total + yrecv[d - 1, h].astype(F32)
        dacc[h * ny + y] = total
    hsend[...] = dacc[(1 - zh) * ny + y].astype(BF16)
    h_copy().start()

    wz_add(0)
    wz_copy(1).start()

    @pl.loop(1, pairs)
    def _(d):
        rz_copy(d, lax.rem(pair + pairs - d, pairs)).wait_recv()

    qs[...] = dot(p_x[...], rz[...].reshape(pairs * blk, fpad), 0, 0).astype(BF16).reshape(
        nx, rowx, fpad
    )

    def rx_copy(d, slot):
        return copy(qs.at[lax.rem(x + d, nx)], rx.at[slot], rx_s.at[d], rx_r.at[d], at_x(d))

    for d in range(1, nx):
        rx_copy(d, x).start()
    rx[x] = qs[x]

    wz_add(1)
    if bits > 2:
        wz_copy(2).start()

    @pl.loop(0, pairs)
    def _(d):
        df_copy(d, 1 - par).wait_recv()

    for i in range(2):
        half = p_z[i * pairs * blk:(i + 1) * pairs * blk, :]
        part = dot(half, zr[i].reshape(pairs * blk, fpad)[:, 0:feat], 0, 0)
        if i == 0:
            ordered = part
        else:
            ordered = ordered + part
    prt[...] = ordered.astype(BF16)
    cols = 256

    @pl.loop(0, ecot.shape[1] // cols)
    def _(i):
        at = pl.ds(pl.multiple_of(i * cols, 128), cols)
        o_ew[:, at] = dot(prt[...], ecot[:, at], 0, 0).astype(BF16)

    for step in range(2, bits):
        wz_add(step)
        if step + 1 < bits:
            wz_copy(step + 1).start()
    base, _ = wz_at(bits)
    o_dw[...] = wz[base][:, 0:wl]

    h_copy().wait_recv()
    for d in range(1, nx):
        rx_copy(d, lax.rem(x + nx - d, nx)).wait_recv()
    expert_sum = dot(rx[...].reshape(nx * rowx, fpad), dmat[...], 0, 0)[0:feat, :]
    dense_sum = dacc[zh * ny + y] + hrecv[...].astype(F32)
    o_in[...] = (expert_sum + dense_sum).astype(BF16)

    for d in range(1, nx):
        dx_copy(d, x).wait_send()
        rx_copy(d, x).wait_send()
        wx_copy(d).wait_send()
    for d in range(1, ny):
        y_copy(d).wait_send()
    h_copy().wait_send()
    for step in range(bits):
        wz_copy(step).wait_send()

    @pl.loop(1, pairs)
    def _(d):
        dz_copy(d, pair).wait_send()
        rz_copy(d, pair).wait_send()

    @pl.loop(0, pairs)
    def _(d):
        df_copy(d, par).wait_send()
        pe_copy(d).wait_send()

    @pl.loop(0, nh * ny)
    def _(k):
        c_copy(k).wait_send()


def body(nx, ny, layer_input, routes, dense_cot, dense_weight, expert_cot, expert_weight):
    nz = lax.axis_size("expert") // nx
    nh = lax.axis_size("dp") // ny
    pairs = nz // 2
    bits = nz.bit_length() - 1
    experts = nx * pairs
    tok, width = layer_input.shape
    feat, cols = expert_weight.shape
    hid = dense_cot.shape[1]
    slots = experts * CAP
    rows = 2 * slots
    fpad = up(feat, 128)
    wl = width // (nx * nz)
    wpad = up(wl, 128)
    rowx, blk = pairs * CAP, nx * CAP

    px = np.zeros((slots, slots), np.float32)
    for p in range(pairs):
        for s in range(nx):
            for c in range(CAP):
                px[p * blk + s * CAP + c, s * rowx + p * CAP + c] = 1
    pz = np.zeros((rows, rows), np.float32)
    for q in range(nz):
        for s in range(nx):
            for c in range(CAP):
                pz[(q % 2) * slots + (q // 2) * blk + s * CAP + c, (s * nz + q) * CAP + c] = 1
    slot = np.arange(slots)
    e_mat = (slot[:, None] // CAP == np.arange(experts)[None, :]).astype(np.float32)
    m_mat = np.broadcast_to((slot % CAP)[:, None], (slots, tok)).astype(np.float32)

    dma = pltpu.SemaphoreType.DMA
    vm = pltpu.VMEM
    groups = nh * ny
    scratch = [
        vm((slots, tok), BF16),
        vm((nx, rowx, fpad), BF16), vm((nx, rowx, fpad), BF16),
        vm((pairs, blk, fpad), BF16), vm((2, pairs, blk, fpad), BF16),
        vm((rows, feat), BF16), vm((2, pairs, blk, fpad), BF16), vm((pairs, blk, fpad), BF16),
        vm((pairs, blk, fpad), BF16), vm((pairs, blk, fpad), BF16),
        vm((nx, rowx, fpad), BF16), vm((nx, rowx, fpad), BF16),
        vm((groups, feat, tok), F32), vm((groups, feat, tok), BF16), vm((groups, feat, tok), BF16),
        vm((ny - 1, nh, feat, tok), BF16), vm((ny - 1, nh, feat, tok), BF16),
        vm((feat, tok), BF16), vm((feat, tok), BF16),
        vm((nx - 1, nz, hid, wpad), BF16), vm((nx - 1, nz, hid, wpad), BF16),
        vm((nz, hid, wpad), F32), vm((nz, hid, wpad), F32),
    ]
    for count in (nx, pairs, pairs, pairs, pairs, nx, groups, ny, 1, nx, bits):
        scratch += [dma((count,)), dma((count,))]
    full = pl.BlockSpec(memory_space=pltpu.VMEM)
    in_t, dw_t, ew_out = pl.pallas_call(
        functools.partial(kernel, (nx, nz, ny, nh)),
        out_shape=(
            jax.ShapeDtypeStruct((feat, tok), BF16),
            jax.ShapeDtypeStruct((hid, wl), F32),
            jax.ShapeDtypeStruct((feat, cols), BF16),
        ),
        in_specs=[full] * 10,
        out_specs=(full, full, full),
        scratch_shapes=scratch,
        compiler_params=pltpu.CompilerParams(
            collective_id=0, has_side_effects=True, vmem_limit_bytes=56 * 1024 * 1024
        ),
    )(
        layer_input, routes.T, dense_cot.T, dense_weight.T, expert_cot, expert_weight,
        jnp.asarray(px, BF16), jnp.asarray(pz, BF16), jnp.asarray(e_mat, BF16),
        jnp.asarray(m_mat, F32),
    )
    return (in_t.T, dw_t.T, ew_out)


def solution(mesh, nx=NX, ny=NY):
    placed = (
        P("expert", None),
        P("expert", None),
        P("expert", ("dp", "tensor")),
        P(None, ("dp", "tensor")),
        P(None, "expert"),
        P(("dp", "tensor"), "expert"),
    )
    return jax.shard_map(
        functools.partial(body, nx, ny),
        mesh=mesh,
        in_specs=placed,
        out_specs=(
            P("expert", ("dp", "tensor")),
            P("expert", ("dp", "tensor")),
            P(("dp", "tensor"), "expert"),
        ),
        check_vma=False,
    )
```

```python
import functools

import jax
import jax.numpy as jnp
import numpy as np
from jax import lax
from jax.experimental import pallas as pl
from jax.experimental.pallas import tpu as pltpu
from jax.sharding import PartitionSpec as P

MESH = pl.DeviceIdType.MESH
F32 = jnp.float32
BF16 = jnp.bfloat16
CAP = 12
NX, NY = 4, 4


def dot(a, b, ca, cb):
    return lax.dot_general(a, b, (((ca,), (cb,)), ((), ())), preferred_element_type=F32)


def rev_bits(q, bits):
    return sum(((q >> b) & 1) << (bits - 1 - b) for b in range(bits))


def up(n, m):
    return -(-n // m) * m


def kernel(
    dims,
    li, rt, cot, wt, ecot, ew, p_x, p_z, e_mat, m_mat,
    o_in, o_dw, o_ew,
    dmat, xs, xr, zs, zr, prt, pz, pin, rs, rz, qs, rx,
    dacc, dsend, dcore, ysend, yrecv, hsend, hrecv,
    wxs, wxr, wz, wzs, wzr, in_sem,
    dx_s, dx_r, dz_s, dz_r, df_s, df_r, pe_s, pe_r, rz_s, rz_r, rx_s, rx_r,
    c_s, c_r, y_s, y_r, h_s, h_r, wx_s, wx_r, wz_s, wz_r,
):
    nx, nz, ny, nh = dims
    pairs = nz // 2
    bits = nz.bit_length() - 1
    feat = ew.shape[0]
    fpad = xs.shape[2]
    wl = o_dw.shape[1]
    win_w = nz * wl
    rowx = pairs * CAP
    dp = lax.axis_index("dp")
    ex = lax.axis_index("expert")
    core = lax.axis_index("tensor")
    x, z = ex // nz, ex % nz
    zh, y = dp // ny, dp % ny
    pair, par = z // 2, z % 2

    def at_x(d):
        return (dp, lax.rem(x + d, nx) * nz + z, core)

    def at_z(zz):
        return (dp, x * nz + zz, core)

    def at_pair(d):
        return at_z(lax.rem(pair + d, pairs) * 2 + par)

    beside = at_z(z + 1 - 2 * par)
    other_core = (dp, ex, 1 - core)

    def at_y(d):
        return (zh * ny + lax.rem(y + d, ny), ex, core)

    other_h = ((1 - zh) * ny + y, ex, core)

    def copy(src, dst, send, recv, dev):
        return pltpu.make_async_remote_copy(
            src_ref=src, dst_ref=dst, send_sem=send, recv_sem=recv,
            device_id=dev, device_id_type=MESH,
        )

    blk = nx * CAP
    higher_z, higher_beside, higher_h = in_sem.at[1], in_sem.at[0], in_sem.at[2]

    def signal(sem, dev):
        pl.semaphore_signal(sem, inc=1, device_id=dev, device_id_type=MESH)

    def at_ring(d):
        around = zh * pairs + pair + d - pairs * ((2 * d + core) // (pairs + 1))
        around = lax.rem(around + nh * pairs, nh * pairs)
        return ((around // pairs) * ny + y, x * nz + lax.rem(around, pairs) * 2 + par, core)

    def at_other_h(k):
        return ((1 - zh) * ny + y, x * nz + k * 2 + par, core)

    same_z = [at_x(d) for d in range(1, nx)] + [other_core] + [at_y(d) for d in range(1, ny)]
    barrier = pltpu.get_barrier_semaphore()
    for dev in same_z:
        signal(barrier, dev)

    @pl.when(par == 0)
    def _():
        signal(barrier, beside)

    @pl.loop(0, pairs)
    def _(k):
        @pl.when(k > pair)
        def _():
            signal(barrier, at_z(2 * k + par))

        @pl.when(zh == 0)
        def _():
            signal(barrier, at_other_h(k))

    pl.semaphore_wait(barrier, len(same_z) + pair + par + zh * pairs)

    @pl.when(par == 1)
    def _():
        signal(higher_beside, beside)

    @pl.loop(0, pairs)
    def _(k):
        @pl.when(k < pair)
        def _():
            signal(higher_z, at_z(2 * k + par))

        @pl.when(zh == 1)
        def _():
            signal(higher_h, at_other_h(k))

    r = rt[...]
    e_row = lax.broadcasted_iota(jnp.int32, (e_mat.shape[1], r.shape[1]), 0)
    member = ((e_row == r[0:1, :]) | (e_row == r[1:2, :])).astype(F32).astype(BF16)
    n_tok = r.shape[1]
    before = lax.broadcasted_iota(jnp.int32, (n_tok, n_tok), 0) < lax.broadcasted_iota(
        jnp.int32, (n_tok, n_tok), 1
    )
    rank = dot(member, before.astype(F32).astype(BF16), 1, 0).astype(BF16)
    is_member = dot(e_mat[...], member, 1, 0)
    ranks = dot(e_mat[...], rank, 1, 0)
    dmat[...] = ((is_member > 0.5) & (ranks == m_mat[...])).astype(F32).astype(BF16)
    chip_w = 2 * feat
    pick_r = lax.broadcasted_iota(jnp.int32, (chip_w, fpad), 0)
    pick_c = lax.broadcasted_iota(jnp.int32, (chip_w, fpad), 1)
    pick = ((pick_r == pick_c + core * feat) & (pick_c < feat)).astype(F32).astype(BF16)

    def features(group):
        window = li[:, pl.ds(pl.multiple_of(group * chip_w, 128), chip_w)]
        return dot(window, pick, 1, 0).astype(BF16)

    mine, theirs = features(dp), features((1 - zh) * ny + y)
    row = lax.broadcasted_iota(jnp.int32, (rowx, fpad), 0)
    to_pair = sum((row >= k * CAP).astype(jnp.int32) for k in range(1, pairs))
    dist = to_pair - pair + jnp.where(to_pair < pair, pairs, 0)
    back = (dist > pairs // 2) | ((dist == pairs // 2) & (core == 1))
    crosses = pair + dist - jnp.where(back, pairs, 0) != to_pair
    for i in range(nx):
        rows_i = dmat[i * rowx:(i + 1) * rowx, :]
        xs[i] = jnp.where(crosses, dot(rows_i, theirs, 1, 0), dot(rows_i, mine, 1, 0)).astype(BF16)
    xr[x] = xs[x]

    def dx_copy(d, slot):
        return copy(xs.at[lax.rem(x + d, nx)], xr.at[slot], dx_s.at[d], dx_r.at[d], at_x(d))

    for d in range(1, nx):
        dx_copy(d, x).start()

    rows_t = ecot.shape[0] // 4
    @pl.loop(0, 4)
    def _(i):
        at = pl.ds(pl.multiple_of(i * rows_t, 16), rows_t)
        prt[at, :] = dot(ecot[at, :], ew[...], 1, 1).astype(BF16)

    pz[:, :, :, feat:] = jnp.zeros((2, pairs, blk, fpad - feat), BF16)
    for i in range(2):
        half = p_z[i * pairs * blk:(i + 1) * pairs * blk, :]
        pz[i, :, :, 0:feat] = dot(half, prt[...], 1, 0).astype(BF16).reshape(pairs, blk, feat)

    def pe_copy(k):
        return copy(pz.at[1 - par, k], pin.at[k], pe_s.at[k], pe_r.at[k], beside)

    @pl.when(par == 0)
    def _():
        pl.semaphore_wait(higher_beside, 1)

    @pl.loop(0, pairs)
    def _(k):
        pe_copy(k).start()

    def c_copy(k):
        return copy(dsend.at[k], dcore.at[k], c_s.at[k], c_r.at[k], other_core)

    @pl.loop(0, nh * ny)
    def _(k):
        part = dot(wt[:, pl.ds(pl.multiple_of(k * chip_w, 128), chip_w)], cot[...], 0, 0)
        low, high = part[0:feat, :], part[feat:, :]
        dacc[k] = jnp.where(core == 0, low, high)
        dsend[k] = jnp.where(core == 0, high, low).astype(BF16)
        c_copy(k).start()

    def wx_copy(d):
        return copy(wxs.at[d - 1], wxr.at[d - 1], wx_s.at[d], wx_r.at[d], at_x(d))

    def wblock(xx):
        w_in = li[:, pl.ds(pl.multiple_of(xx * win_w, 128), win_w)]
        return dot(cot[...], w_in, 1, 0)

    for d in range(1, nx):
        got = wblock(lax.rem(x + d, nx))
        for q in range(nz):
            wxs[d - 1, rev_bits(q, bits), :, 0:wl] = got[:, q * wl:(q + 1) * wl].astype(BF16)
        wxs[d - 1, :, :, wl:] = jnp.zeros((nz, wxs.shape[2], wxs.shape[3] - wl), BF16)
        wx_copy(d).start()
    got = wblock(x)
    for q in range(nz):
        wz[rev_bits(q, bits), :, 0:wl] = got[:, q * wl:(q + 1) * wl]
    wz[:, :, wl:] = jnp.zeros((nz, wz.shape[1], wz.shape[2] - wl), F32)

    def y_copy(d):
        return copy(ysend.at[d - 1], yrecv.at[d - 1], y_s.at[d], y_r.at[d], at_y(d))

    def core_sum(k):
        c_copy(k).wait_recv()
        return dacc[k] + dcore[k].astype(F32)

    for d in range(1, ny):
        for h in range(nh):
            ysend[d - 1, h] = core_sum(h * ny + lax.rem(y + d, ny)).astype(BF16)
        y_copy(d).start()
    for h in range(nh):
        dacc[h * ny + y] = core_sum(h * ny + y)

    for d in range(1, nx):
        dx_copy(d, lax.rem(x + nx - d, nx)).wait_recv()
    zs[...] = dot(p_x[...], xr[...].reshape(nx * rowx, fpad), 1, 0).astype(BF16).reshape(
        pairs, blk, fpad
    )

    def dz_copy(d, slot):
        return copy(
            zs.at[lax.rem(pair + d, pairs)], zr.at[par, slot], dz_s.at[d], dz_r.at[d], at_ring(d)
        )

    def df_copy(d, side):
        slot = lax.rem(pair + pairs - d, pairs)
        return copy(zr.at[side, slot], zr.at[side, slot], df_s.at[d], df_r.at[d], beside)

    zr[par, pair] = zs[pair]
    df_copy(0, par).start()

    @pl.when(pair < pairs - 1)
    def _():
        pl.semaphore_wait(higher_z, pairs - 1 - pair)

    def rz_copy(d, slot):
        return copy(
            rs.at[lax.rem(pair + d, pairs)], rz.at[slot], rz_s.at[d], rz_r.at[d], at_pair(d)
        )

    @pl.loop(1, pairs)
    def _(d):
        k = lax.rem(pair + d, pairs)
        pe_copy(k).wait_recv()
        rs[k] = (pz[par, k].astype(F32) + pin[k].astype(F32)).astype(BF16)
        rz_copy(d, pair).start()

    pe_copy(pair).wait_recv()
    rz[pair] = (pz[par, pair].astype(F32) + pin[pair].astype(F32)).astype(BF16)

    @pl.loop(1, pairs)
    def _(d):
        @pl.when(at_ring(d)[0] == dp)
        def _():
            dz_copy(d, pair).start()

    def wz_at(step):
        base, size = 0, nz
        for b in range(step):
            size = size // 2
            base = base + ((z // (1 << b)) % 2) * size
        return base, size

    def wz_copy(step):
        size = nz >> (step + 1)
        at = pl.ds(nz - 2 * size, size)
        bit = (z // (1 << step)) % 2
        partner = at_z(z + (1 - 2 * bit) * (1 << step))
        return copy(wzs.at[at], wzr.at[at], wz_s.at[step], wz_r.at[step], partner)

    def wz_step(step, total):
        base, size = wz_at(step)
        if step < bits:
            size = size // 2
            bit = (z // (1 << step)) % 2
            away, base = base + (1 - bit) * size, base + bit * size

            @pl.loop(0, size)
            def _(i):
                wzs[nz - 2 * size + i] = total(away + i).astype(BF16)

            wz_copy(step).start()

        @pl.loop(0, size)
        def _(i):
            wz[base + i] = total(base + i)

    def wz_next(step):
        wz_copy(step - 1).wait_recv()
        base, size = wz_at(step)
        land = nz - 2 * size
        wz_step(step, lambda i: wz[i] + wzr[land + i - base].astype(F32))

    for d in range(1, nx):
        wx_copy(d).wait_recv()

    def over_x(i):
        total = wz[i]
        for d in range(1, nx):
            total = total + wxr[d - 1, i].astype(F32)
        return total

    wz_step(0, over_x)

    def h_copy():
        return copy(hsend, hrecv, h_s.at[0], h_r.at[0], other_h)

    for d in range(1, ny):
        y_copy(d).wait_recv()
    for h in range(nh):
        total = dacc[h * ny + y]
        for d in range(1, ny):
            total = total + yrecv[d - 1, h].astype(F32)
        dacc[h * ny + y] = total
    hsend[...] = dacc[(1 - zh) * ny + y].astype(BF16)

    @pl.when(zh == 0)
    def _():
        pl.semaphore_wait(higher_h, pairs)

    @pl.loop(1, pairs)
    def _(d):
        @pl.when(at_ring(d)[0] != dp)
        def _():
            dz_copy(d, pair).start()

    h_copy().start()

    @pl.loop(1, pairs)
    def _(d):
        dz_copy(d, lax.rem(pair + pairs - d, pairs)).wait_recv()
        df_copy(d, par).start()

    wz_next(1)

    @pl.loop(1, pairs)
    def _(d):
        rz_copy(d, lax.rem(pair + pairs - d, pairs)).wait_recv()

    qs[...] = dot(p_x[...], rz[...].reshape(pairs * blk, fpad), 0, 0).astype(BF16).reshape(
        nx, rowx, fpad
    )

    def rx_copy(d, slot):
        return copy(qs.at[lax.rem(x + d, nx)], rx.at[slot], rx_s.at[d], rx_r.at[d], at_x(d))

    for d in range(1, nx):
        rx_copy(d, x).start()
    rx[x] = qs[x]

    if bits > 2:
        wz_next(2)

    @pl.loop(0, pairs)
    def _(d):
        df_copy(d, 1 - par).wait_recv()

    for i in range(2):
        half = p_z[i * pairs * blk:(i + 1) * pairs * blk, :]
        part = dot(half, zr[i].reshape(pairs * blk, fpad)[:, 0:feat], 0, 0)
        if i == 0:
            ordered = part
        else:
            ordered = ordered + part
    prt[...] = ordered.astype(BF16)
    cols = 256

    @pl.loop(0, ecot.shape[1] // cols)
    def _(i):
        at = pl.ds(pl.multiple_of(i * cols, 128), cols)
        o_ew[:, at] = dot(prt[...], ecot[:, at], 0, 0).astype(BF16)

    for step in range(min(3, bits), bits + 1):
        wz_next(step)
    base, _ = wz_at(bits)
    o_dw[...] = wz[base][:, 0:wl]

    h_copy().wait_recv()
    for d in range(1, nx):
        rx_copy(d, lax.rem(x + nx - d, nx)).wait_recv()
    expert_sum = dot(rx[...].reshape(nx * rowx, fpad), dmat[...], 0, 0)[0:feat, :]
    dense_sum = dacc[zh * ny + y] + hrecv[...].astype(F32)
    o_in[...] = (expert_sum + dense_sum).astype(BF16)

    for d in range(1, nx):
        dx_copy(d, x).wait_send()
        rx_copy(d, x).wait_send()
        wx_copy(d).wait_send()
    for d in range(1, ny):
        y_copy(d).wait_send()
    h_copy().wait_send()
    for step in range(bits):
        wz_copy(step).wait_send()

    @pl.loop(1, pairs)
    def _(d):
        dz_copy(d, pair).wait_send()
        rz_copy(d, pair).wait_send()

    @pl.loop(0, pairs)
    def _(d):
        df_copy(d, par).wait_send()
        pe_copy(d).wait_send()

    @pl.loop(0, nh * ny)
    def _(k):
        c_copy(k).wait_send()


def body(nx, ny, layer_input, routes, dense_cot, dense_weight, expert_cot, expert_weight):
    nz = lax.axis_size("expert") // nx
    nh = lax.axis_size("dp") // ny
    pairs = nz // 2
    bits = nz.bit_length() - 1
    experts = nx * pairs
    tok, width = layer_input.shape
    feat, cols = expert_weight.shape
    hid = dense_cot.shape[1]
    slots = experts * CAP
    rows = 2 * slots
    fpad = up(feat, 128)
    wl = width // (nx * nz)
    wpad = up(wl, 128)
    rowx, blk = pairs * CAP, nx * CAP

    px = np.zeros((slots, slots), np.float32)
    for p in range(pairs):
        for s in range(nx):
            for c in range(CAP):
                px[p * blk + s * CAP + c, s * rowx + p * CAP + c] = 1
    pz = np.zeros((rows, rows), np.float32)
    for q in range(nz):
        for s in range(nx):
            for c in range(CAP):
                pz[(q % 2) * slots + (q // 2) * blk + s * CAP + c, (s * nz + q) * CAP + c] = 1
    slot = np.arange(slots)
    e_mat = (slot[:, None] // CAP == np.arange(experts)[None, :]).astype(np.float32)
    m_mat = np.broadcast_to((slot % CAP)[:, None], (slots, tok)).astype(np.float32)

    dma = pltpu.SemaphoreType.DMA
    vm = pltpu.VMEM
    groups = nh * ny
    scratch = [
        vm((slots, tok), BF16),
        vm((nx, rowx, fpad), BF16), vm((nx, rowx, fpad), BF16),
        vm((pairs, blk, fpad), BF16), vm((2, pairs, blk, fpad), BF16),
        vm((rows, feat), BF16), vm((2, pairs, blk, fpad), BF16), vm((pairs, blk, fpad), BF16),
        vm((pairs, blk, fpad), BF16), vm((pairs, blk, fpad), BF16),
        vm((nx, rowx, fpad), BF16), vm((nx, rowx, fpad), BF16),
        vm((groups, feat, tok), F32), vm((groups, feat, tok), BF16), vm((groups, feat, tok), BF16),
        vm((ny - 1, nh, feat, tok), BF16), vm((ny - 1, nh, feat, tok), BF16),
        vm((feat, tok), BF16), vm((feat, tok), BF16),
        vm((nx - 1, nz, hid, wpad), BF16), vm((nx - 1, nz, hid, wpad), BF16),
        vm((nz, hid, wpad), F32), vm((nz, hid, wpad), BF16), vm((nz, hid, wpad), BF16),
        pltpu.SemaphoreType.REGULAR((3,)),
    ]
    for count in (nx, pairs, pairs, pairs, pairs, nx, groups, ny, 1, nx, bits):
        scratch += [dma((count,)), dma((count,))]
    full = pl.BlockSpec(memory_space=pltpu.VMEM)
    in_t, dw_t, ew_out = pl.pallas_call(
        functools.partial(kernel, (nx, nz, ny, nh)),
        out_shape=(
            jax.ShapeDtypeStruct((feat, tok), BF16),
            jax.ShapeDtypeStruct((hid, wl), F32),
            jax.ShapeDtypeStruct((feat, cols), BF16),
        ),
        in_specs=[full] * 10,
        out_specs=(full, full, full),
        scratch_shapes=scratch,
        compiler_params=pltpu.CompilerParams(
            collective_id=0, has_side_effects=True, vmem_limit_bytes=56 * 1024 * 1024
        ),
    )(
        layer_input, routes.T, dense_cot.T, dense_weight.T, expert_cot, expert_weight,
        jnp.asarray(px, BF16), jnp.asarray(pz, BF16), jnp.asarray(e_mat, BF16),
        jnp.asarray(m_mat, F32),
    )
    return (in_t.T, dw_t.T, ew_out)


def solution(mesh, nx=NX, ny=NY):
    placed = (
        P("expert", None),
        P("expert", None),
        P("expert", ("dp", "tensor")),
        P(None, ("dp", "tensor")),
        P(None, "expert"),
        P(("dp", "tensor"), "expert"),
    )
    return jax.shard_map(
        functools.partial(body, nx, ny),
        mesh=mesh,
        in_specs=placed,
        out_specs=(
            P("expert", ("dp", "tensor")),
            P("expert", ("dp", "tensor")),
            P(("dp", "tensor"), "expert"),
        ),
        check_vma=False,
    )
```

```python
import functools

import jax
import jax.numpy as jnp
import numpy as np
from jax import lax
from jax.experimental import pallas as pl
from jax.experimental.pallas import tpu as pltpu
from jax.sharding import PartitionSpec as P

MESH = pl.DeviceIdType.MESH
F32 = jnp.float32
BF16 = jnp.bfloat16
CAP = 12
NX, NY = 4, 4


def dot(a, b, ca, cb):
    return lax.dot_general(a, b, (((ca,), (cb,)), ((), ())), preferred_element_type=F32)


def rev_bits(q, bits):
    return sum(((q >> b) & 1) << (bits - 1 - b) for b in range(bits))


def up(n, m):
    return -(-n // m) * m


def kernel(
    dims,
    li, rt, cot, wt_hbm, ecot_hbm, ew_hbm, p_x, p_z_hbm, e_mat, m_mat,
    o_in, o_dw, o_ew,
    dmat, xs, xr, zs, zr, prt, pz, pin, rs, rz, qs, rx,
    dacc, dsend, dcore, ysend, yrecv, hsend, hrecv,
    wxs, wxr, wz, wzs, wzr, in_sem, wt, ecot, ew, p_z, load_s,
    dx_s, dx_r, dz_s, dz_r, df_s, df_r, pe_s, pe_r, rz_s, rz_r, rx_s, rx_r,
    c_s, c_r, y_s, y_r, h_s, h_r, wx_s, wx_r, wz_s, wz_r,
):
    nx, nz, ny, nh = dims
    from_hbm = ((ecot_hbm, ecot), (ew_hbm, ew), (p_z_hbm, p_z), (wt_hbm, wt))
    loads = [pltpu.make_async_copy(a, b, load_s.at[i]) for i, (a, b) in enumerate(from_hbm)]
    for load in loads:
        load.start()
    pairs = nz // 2
    bits = nz.bit_length() - 1
    feat = ew.shape[0]
    fpad = xs.shape[2]
    wl = o_dw.shape[1]
    win_w = nz * wl
    rowx = pairs * CAP
    dp = lax.axis_index("dp")
    ex = lax.axis_index("expert")
    core = lax.axis_index("tensor")
    x, z = ex // nz, ex % nz
    zh, y = dp // ny, dp % ny
    pair, par = z // 2, z % 2

    def at_x(d):
        return (dp, lax.rem(x + d, nx) * nz + z, core)

    def at_z(zz):
        return (dp, x * nz + zz, core)

    beside = at_z(z + 1 - 2 * par)
    other_core = (dp, ex, 1 - core)

    def at_y(d):
        return (zh * ny + lax.rem(y + d, ny), ex, core)

    other_h = ((1 - zh) * ny + y, ex, core)

    def copy(src, dst, send, recv, dev):
        return pltpu.make_async_remote_copy(
            src_ref=src, dst_ref=dst, send_sem=send, recv_sem=recv,
            device_id=dev, device_id_type=MESH,
        )

    blk = nx * CAP
    higher_z, higher_beside, higher_h = in_sem.at[1], in_sem.at[0], in_sem.at[2]

    def signal(sem, dev):
        pl.semaphore_signal(sem, inc=1, device_id=dev, device_id_type=MESH)

    def at_ring(d):
        around = zh * pairs + pair + d - pairs * goes_back(d)
        around = lax.rem(around + nh * pairs, nh * pairs)
        first = lax.rem(around, pairs) * 2 + goes_back(d)
        return ((around // pairs) * ny + y, x * nz + first, core)

    def goes_back(d):
        return (2 * d + core) // (pairs + 1)

    def far_first(i):
        return pairs // 2 + (i // 2) * (1 - 2 * (i % 2))

    def at_other_h(zz):
        return ((1 - zh) * ny + y, x * nz + zz, core)

    same_z = [at_x(d) for d in range(1, nx)] + [other_core] + [at_y(d) for d in range(1, ny)]
    barrier = pltpu.get_barrier_semaphore()
    for dev in same_z:
        signal(barrier, dev)

    @pl.when(par == 0)
    def _():
        signal(barrier, beside)

    @pl.loop(0, nz)
    def _(zz):
        @pl.when(zz // 2 > pair)
        def _():
            signal(barrier, at_z(zz))

        @pl.when(zh == 0)
        def _():
            signal(barrier, at_other_h(zz))

    pl.semaphore_wait(barrier, len(same_z) + 2 * pair + par + zh * nz)

    @pl.when(par == 1)
    def _():
        signal(higher_beside, beside)

    @pl.loop(0, nz)
    def _(zz):
        @pl.when(zz // 2 < pair)
        def _():
            signal(higher_z, at_z(zz))

        @pl.when(zh == 1)
        def _():
            signal(higher_h, at_other_h(zz))

    r = rt[...]
    e_row = lax.broadcasted_iota(jnp.int32, (e_mat.shape[1], r.shape[1]), 0)
    member = ((e_row == r[0:1, :]) | (e_row == r[1:2, :])).astype(F32).astype(BF16)
    n_tok = r.shape[1]
    before = lax.broadcasted_iota(jnp.int32, (n_tok, n_tok), 0) < lax.broadcasted_iota(
        jnp.int32, (n_tok, n_tok), 1
    )
    rank = dot(member, before.astype(F32).astype(BF16), 1, 0).astype(BF16)
    is_member = dot(e_mat[...], member, 1, 0)
    ranks = dot(e_mat[...], rank, 1, 0)
    dmat[...] = ((is_member > 0.5) & (ranks == m_mat[...])).astype(F32).astype(BF16)
    chip_w = 2 * feat
    pick_r = lax.broadcasted_iota(jnp.int32, (chip_w, fpad), 0)
    pick_c = lax.broadcasted_iota(jnp.int32, (chip_w, fpad), 1)
    pick = ((pick_r == pick_c + core * feat) & (pick_c < feat)).astype(F32).astype(BF16)

    def features(group):
        window = li[:, pl.ds(pl.multiple_of(group * chip_w, 128), chip_w)]
        return dot(window, pick, 1, 0).astype(BF16)

    mine, theirs = features(dp), features((1 - zh) * ny + y)
    row = lax.broadcasted_iota(jnp.int32, (rowx, fpad), 0)
    to_pair = sum((row >= k * CAP).astype(jnp.int32) for k in range(1, pairs))
    dist = to_pair - pair + jnp.where(to_pair < pair, pairs, 0)
    back = (dist > pairs // 2) | ((dist == pairs // 2) & (core == 1))
    crosses = pair + dist - jnp.where(back, pairs, 0) != to_pair
    for i in range(nx):
        rows_i = dmat[i * rowx:(i + 1) * rowx, :]
        xs[i] = jnp.where(crosses, dot(rows_i, theirs, 1, 0), dot(rows_i, mine, 1, 0)).astype(BF16)
    xr[x] = xs[x]

    def dx_copy(d, slot):
        return copy(xs.at[lax.rem(x + d, nx)], xr.at[slot], dx_s.at[d], dx_r.at[d], at_x(d))

    for d in range(1, nx):
        dx_copy(d, x).start()

    for load in loads[:3]:
        load.wait()
    rows_t = ecot.shape[0] // 4
    @pl.loop(0, 4)
    def _(i):
        at = pl.ds(pl.multiple_of(i * rows_t, 16), rows_t)
        prt[at, :] = dot(ecot[at, :], ew[...], 1, 1).astype(BF16)

    pz[:, :, :, feat:] = jnp.zeros((2, pairs, blk, fpad - feat), BF16)
    for i in range(2):
        half = p_z[i * pairs * blk:(i + 1) * pairs * blk, :]
        pz[i, :, :, 0:feat] = dot(half, prt[...], 1, 0).astype(BF16).reshape(pairs, blk, feat)

    def pe_copy(sp, k):
        i = 2 * k + sp
        return copy(pz.at[sp, k], pin.at[sp, k], pe_s.at[i], pe_r.at[i], beside)

    def on_side(side, k):
        return (k - pair) * (2 * side - 1) > 0

    def each_on(side, fn):
        @pl.loop(0, pairs)
        def _(i):
            k = i + side * (pairs - 1 - 2 * i)

            @pl.when(on_side(side, k))
            def _():
                fn(0, k)
                fn(1, k)

    @pl.when(par == 0)
    def _():
        pl.semaphore_wait(higher_beside, 1)

    each_on(1 - par, lambda sp, k: pe_copy(sp, k).start())
    pe_copy(1 - par, pair).start()

    for d in range(1, nx):
        dx_copy(d, lax.rem(x + nx - d, nx)).wait_recv()
    zs[...] = dot(p_x[...], xr[...].reshape(nx * rowx, fpad), 1, 0).astype(BF16).reshape(
        pairs, blk, fpad
    )

    def dz_copy(d, side, slot):
        return copy(
            zs.at[lax.rem(pair + d, pairs)], zr.at[side, slot],
            dz_s.at[d], dz_r.at[2 * d + side], at_ring(d),
        )

    def df_copy(d, side):
        slot = lax.rem(pair + pairs - d, pairs)
        i = 2 * d + side
        return copy(zr.at[side, slot], zr.at[side, slot], df_s.at[i], df_r.at[i], beside)

    def each_way(back, fn):
        @pl.loop(1, pairs)
        def _(i):
            d = far_first(i)

            @pl.when(goes_back(d) == back)
            def _():
                fn(d, 0)
                fn(d, 1)

    zr[par, pair] = zs[pair]
    df_copy(0, par).start()

    def send_rows(same_h):
        @pl.loop(1, pairs)
        def _(i):
            d = far_first(i)

            @pl.when((at_ring(d)[0] == dp) == same_h)
            def _():
                dz_copy(d, par, pair).start()

    def wait_higher_z():
        @pl.when(pair < pairs - 1)
        def _():
            pl.semaphore_wait(higher_z, 2 * (pairs - 1 - pair))

    @pl.when(zh == 1)
    def _():
        wait_higher_z()
        send_rows(True)
        send_rows(False)

    loads[3].wait()

    def c_copy(k):
        return copy(dsend.at[k], dcore.at[k], c_s.at[k], c_r.at[k], other_core)

    @pl.loop(0, nh * ny)
    def _(k):
        part = dot(wt[:, pl.ds(pl.multiple_of(k * chip_w, 128), chip_w)], cot[...], 0, 0)
        low, high = part[0:feat, :], part[feat:, :]
        dacc[k] = jnp.where(core == 0, low, high)
        dsend[k] = jnp.where(core == 0, high, low).astype(BF16)
        c_copy(k).start()

    def wx_copy(d):
        return copy(wxs.at[d - 1], wxr.at[d - 1], wx_s.at[d], wx_r.at[d], at_x(d))

    def wblock(xx):
        w_in = li[:, pl.ds(pl.multiple_of(xx * win_w, 128), win_w)]
        return dot(cot[...], w_in, 1, 0)

    for d in range(1, nx):
        got = wblock(lax.rem(x + d, nx))
        for q in range(nz):
            wxs[d - 1, rev_bits(q, bits), :, 0:wl] = got[:, q * wl:(q + 1) * wl].astype(BF16)
        wxs[d - 1, :, :, wl:] = jnp.zeros((nz, wxs.shape[2], wxs.shape[3] - wl), BF16)
        wx_copy(d).start()
    got = wblock(x)
    for q in range(nz):
        wz[rev_bits(q, bits), :, 0:wl] = got[:, q * wl:(q + 1) * wl]
    wz[:, :, wl:] = jnp.zeros((nz, wz.shape[1], wz.shape[2] - wl), F32)

    def y_copy(d):
        return copy(ysend.at[d - 1], yrecv.at[d - 1], y_s.at[d], y_r.at[d], at_y(d))

    def core_sum(k):
        c_copy(k).wait_recv()
        return dacc[k] + dcore[k].astype(F32)

    for d in range(1, ny):
        for h in range(nh):
            ysend[d - 1, h] = core_sum(h * ny + lax.rem(y + d, ny)).astype(BF16)
        y_copy(d).start()
    for h in range(nh):
        dacc[h * ny + y] = core_sum(h * ny + y)

    @pl.when(zh == 0)
    def _():
        wait_higher_z()
        send_rows(True)

    def rz_copy(sp, k, slot):
        return copy(rs.at[sp, k], rz.at[slot], rz_s.at[2 * k + sp], rz_r.at[slot], at_z(2 * k + sp))

    def pair_sum(sp, k):
        pe_copy(sp, k).wait_recv()
        return (pz[sp, k].astype(F32) + pin[sp, k].astype(F32)).astype(BF16)

    def return_rows(sp, k):
        rs[sp, k] = pair_sum(sp, k)
        rz_copy(sp, k, pair).start()

    each_on(par, return_rows)
    rz[pair] = pair_sum(par, pair)

    @pl.when(zh == 0)
    def _():
        pl.semaphore_wait(higher_h, nz)
        send_rows(False)

    def h_copy():
        return copy(hsend, hrecv, h_s.at[0], h_r.at[0], other_h)

    for d in range(1, ny):
        y_copy(d).wait_recv()
    for h in range(nh):
        total = dacc[h * ny + y]
        for d in range(1, ny):
            total = total + yrecv[d - 1, h].astype(F32)
        dacc[h * ny + y] = total
    hsend[...] = dacc[(1 - zh) * ny + y].astype(BF16)

    h_copy().start()

    def wz_at(step):
        base, size = 0, nz
        for b in range(step):
            size = size // 2
            base = base + ((z // (1 << b)) % 2) * size
        return base, size

    def wz_copy(step):
        size = nz >> (step + 1)
        at = pl.ds(nz - 2 * size, size)
        bit = (z // (1 << step)) % 2
        partner = at_z(z + (1 - 2 * bit) * (1 << step))
        return copy(wzs.at[at], wzr.at[at], wz_s.at[step], wz_r.at[step], partner)

    def wz_step(step, total):
        base, size = wz_at(step)
        if step < bits:
            size = size // 2
            bit = (z // (1 << step)) % 2
            away, base = base + (1 - bit) * size, base + bit * size

            @pl.loop(0, size)
            def _(i):
                wzs[nz - 2 * size + i] = total(away + i).astype(BF16)

            wz_copy(step).start()

        @pl.loop(0, size)
        def _(i):
            wz[base + i] = total(base + i)

    def wz_next(step):
        wz_copy(step - 1).wait_recv()
        base, size = wz_at(step)
        land = nz - 2 * size
        wz_step(step, lambda i: wz[i] + wzr[land + i - base].astype(F32))

    for d in range(1, nx):
        wx_copy(d).wait_recv()

    def over_x(i):
        total = wz[i]
        for d in range(1, nx):
            total = total + wxr[d - 1, i].astype(F32)
        return total

    wz_step(0, over_x)

    def forward(d, side):
        dz_copy(d, side, lax.rem(pair + pairs - d, pairs)).wait_recv()
        df_copy(d, side).start()

    each_way(par, forward)

    wz_next(1)

    @pl.loop(0, pairs)
    def _(k):
        @pl.when(k != pair)
        def _():
            rz_copy(par, k, k).wait_recv()

    qs[...] = dot(p_x[...], rz[...].reshape(pairs * blk, fpad), 0, 0).astype(BF16).reshape(
        nx, rowx, fpad
    )

    def rx_copy(d, slot):
        return copy(qs.at[lax.rem(x + d, nx)], rx.at[slot], rx_s.at[d], rx_r.at[d], at_x(d))

    for d in range(1, nx):
        rx_copy(d, x).start()
    rx[x] = qs[x]

    if bits > 2:
        wz_next(2)

    each_way(1 - par, lambda d, side: df_copy(d, side).wait_recv())
    df_copy(0, 1 - par).wait_recv()

    for i in range(2):
        half = p_z[i * pairs * blk:(i + 1) * pairs * blk, :]
        part = dot(half, zr[i].reshape(pairs * blk, fpad)[:, 0:feat], 0, 0)
        if i == 0:
            ordered = part
        else:
            ordered = ordered + part
    prt[...] = ordered.astype(BF16)
    cols = 256

    @pl.loop(0, ecot.shape[1] // cols)
    def _(i):
        at = pl.ds(pl.multiple_of(i * cols, 128), cols)
        o_ew[:, at] = dot(prt[...], ecot[:, at], 0, 0).astype(BF16)

    for step in range(min(3, bits), bits + 1):
        wz_next(step)
    base, _ = wz_at(bits)
    o_dw[...] = wz[base][:, 0:wl]

    h_copy().wait_recv()
    for d in range(1, nx):
        rx_copy(d, lax.rem(x + nx - d, nx)).wait_recv()
    expert_sum = dot(rx[...].reshape(nx * rowx, fpad), dmat[...], 0, 0)[0:feat, :]
    dense_sum = dacc[zh * ny + y] + hrecv[...].astype(F32)
    o_in[...] = (expert_sum + dense_sum).astype(BF16)

    for d in range(1, nx):
        dx_copy(d, x).wait_send()
        rx_copy(d, x).wait_send()
        wx_copy(d).wait_send()
    for d in range(1, ny):
        y_copy(d).wait_send()
    h_copy().wait_send()
    for step in range(bits):
        wz_copy(step).wait_send()

    @pl.loop(1, pairs)
    def _(d):
        dz_copy(d, par, pair).wait_send()

    each_way(par, lambda d, side: df_copy(d, side).wait_send())
    df_copy(0, par).wait_send()
    each_on(1 - par, lambda sp, k: pe_copy(sp, k).wait_send())
    pe_copy(1 - par, pair).wait_send()
    each_on(par, lambda sp, k: rz_copy(sp, k, pair).wait_send())

    @pl.loop(0, nh * ny)
    def _(k):
        c_copy(k).wait_send()


def body(nx, ny, layer_input, routes, dense_cot, dense_weight, expert_cot, expert_weight):
    nz = lax.axis_size("expert") // nx
    nh = lax.axis_size("dp") // ny
    pairs = nz // 2
    bits = nz.bit_length() - 1
    experts = nx * pairs
    tok, width = layer_input.shape
    feat, cols = expert_weight.shape
    hid = dense_cot.shape[1]
    slots = experts * CAP
    rows = 2 * slots
    fpad = up(feat, 128)
    wl = width // (nx * nz)
    wpad = up(wl, 128)
    rowx, blk = pairs * CAP, nx * CAP

    px = np.zeros((slots, slots), np.float32)
    for p in range(pairs):
        for s in range(nx):
            for c in range(CAP):
                px[p * blk + s * CAP + c, s * rowx + p * CAP + c] = 1
    pz = np.zeros((rows, rows), np.float32)
    for q in range(nz):
        for s in range(nx):
            for c in range(CAP):
                pz[(q % 2) * slots + (q // 2) * blk + s * CAP + c, (s * nz + q) * CAP + c] = 1
    slot = np.arange(slots)
    e_mat = (slot[:, None] // CAP == np.arange(experts)[None, :]).astype(np.float32)
    m_mat = np.broadcast_to((slot % CAP)[:, None], (slots, tok)).astype(np.float32)

    dma = pltpu.SemaphoreType.DMA
    vm = pltpu.VMEM
    groups = nh * ny
    scratch = [
        vm((slots, tok), BF16),
        vm((nx, rowx, fpad), BF16), vm((nx, rowx, fpad), BF16),
        vm((pairs, blk, fpad), BF16), vm((2, pairs, blk, fpad), BF16),
        vm((rows, feat), BF16), vm((2, pairs, blk, fpad), BF16), vm((2, pairs, blk, fpad), BF16),
        vm((2, pairs, blk, fpad), BF16), vm((pairs, blk, fpad), BF16),
        vm((nx, rowx, fpad), BF16), vm((nx, rowx, fpad), BF16),
        vm((groups, feat, tok), F32), vm((groups, feat, tok), BF16), vm((groups, feat, tok), BF16),
        vm((ny - 1, nh, feat, tok), BF16), vm((ny - 1, nh, feat, tok), BF16),
        vm((feat, tok), BF16), vm((feat, tok), BF16),
        vm((nx - 1, nz, hid, wpad), BF16), vm((nx - 1, nz, hid, wpad), BF16),
        vm((nz, hid, wpad), F32), vm((nz, hid, wpad), BF16), vm((nz, hid, wpad), BF16),
        pltpu.SemaphoreType.REGULAR((3,)),
        vm((hid, width), BF16), vm((rows, cols), BF16), vm((feat, cols), BF16),
        vm((rows, rows), BF16), dma((4,)),
    ]
    for count in (nx, nz, nz, nz, nz, nx, groups, ny, 1, nx, bits):
        scratch += [dma((count,)), dma((count,))]
    full = pl.BlockSpec(memory_space=pltpu.VMEM)
    hbm = pl.BlockSpec(memory_space=pl.ANY)
    in_t, dw_t, ew_out = pl.pallas_call(
        functools.partial(kernel, (nx, nz, ny, nh)),
        out_shape=(
            jax.ShapeDtypeStruct((feat, tok), BF16),
            jax.ShapeDtypeStruct((hid, wl), F32),
            jax.ShapeDtypeStruct((feat, cols), BF16),
        ),
        in_specs=[full] * 3 + [hbm] * 3 + [full, hbm, full, full],
        out_specs=(full, full, full),
        scratch_shapes=scratch,
        compiler_params=pltpu.CompilerParams(
            collective_id=0, has_side_effects=True, vmem_limit_bytes=56 * 1024 * 1024
        ),
    )(
        layer_input, routes.T, dense_cot.T, dense_weight.T, expert_cot, expert_weight,
        jnp.asarray(px, BF16), jnp.asarray(pz, BF16), jnp.asarray(e_mat, BF16),
        jnp.asarray(m_mat, F32),
    )
    return (in_t.T, dw_t.T, ew_out)


def solution(mesh, nx=NX, ny=NY):
    placed = (
        P("expert", None),
        P("expert", None),
        P("expert", ("dp", "tensor")),
        P(None, ("dp", "tensor")),
        P(None, "expert"),
        P(("dp", "tensor"), "expert"),
    )
    return jax.shard_map(
        functools.partial(body, nx, ny),
        mesh=mesh,
        in_specs=placed,
        out_specs=(
            P("expert", ("dp", "tensor")),
            P("expert", ("dp", "tensor")),
            P(("dp", "tensor"), "expert"),
        ),
        check_vma=False,
    )
```

```python
import functools

import jax
import jax.numpy as jnp
import numpy as np
from jax import lax
from jax.experimental import pallas as pl
from jax.experimental.pallas import tpu as pltpu
from jax.sharding import PartitionSpec as P

MESH = pl.DeviceIdType.MESH
F32 = jnp.float32
BF16 = jnp.bfloat16
CAP = 12
NX, NY = 4, 4


def dot(a, b, ca, cb):
    return lax.dot_general(a, b, (((ca,), (cb,)), ((), ())), preferred_element_type=F32)


def rev_bits(q, bits):
    return sum(((q >> b) & 1) << (bits - 1 - b) for b in range(bits))


def up(n, m):
    return -(-n // m) * m


def pack(v, blk, feat):
    n = v.shape[0] // blk
    whole, rest = feat // 128, feat % 128
    v = v.reshape(n, blk, v.shape[1])
    parts = [v[:, :, t * 128:(t + 1) * 128] for t in range(whole)]
    if rest:
        half = blk // 2
        last = v[:, :, whole * 128:feat]
        parts.append(jnp.concatenate([last[:, :half, :], last[:, half:, :]], axis=2))
        parts.append(jnp.zeros((n, packed_rows(blk, feat) - whole * blk - half, 128), v.dtype))
    return jnp.concatenate(parts, axis=1)


def unpack(v, blk, feat):
    n = v.shape[0]
    whole, rest = feat // 128, feat % 128
    parts = [v[:, t * blk:(t + 1) * blk, :].reshape(n * blk, 128) for t in range(whole)]
    if rest:
        half = blk // 2
        last = v[:, whole * blk:, :].astype(F32)
        last = jnp.concatenate([last[:, :half, :rest], last[:, :half, rest:]], axis=1)
        parts.append(last.reshape(n * blk, rest).astype(v.dtype))
    return jnp.concatenate(parts, axis=1) if len(parts) > 1 else parts[0]


def packed_rows(blk, feat):
    return feat // 128 * blk + (up(blk // 2, 16) if feat % 128 else 0)


def kernel(
    dims,
    li, rt, cot, wt_hbm, ecot_hbm, ew_hbm, p_x, p_z_hbm, e_mat, m_mat,
    o_in, o_dw, o_ew,
    dmat, xs, xr, zs, zr, prt, pz, pin, rs, rz, qs, rx,
    dacc, dsend, dcore, ysend, yrecv, hsend, hrecv,
    wxs, wxr, wz, wzs, wzr, in_sem, wt, ecot, ew, p_z, load_s,
    dx_s, dx_r, dz_s, dz_r, df_s, df_r, pe_s, pe_r, rz_s, rz_r, rx_s, rx_r,
    c_s, c_r, y_s, y_r, h_s, h_r, wx_s, wx_r, wz_s, wz_r,
):
    nx, nz, ny, nh = dims
    from_hbm = ((ecot_hbm, ecot), (ew_hbm, ew), (p_z_hbm, p_z), (wt_hbm, wt))
    loads = [pltpu.make_async_copy(a, b, load_s.at[i]) for i, (a, b) in enumerate(from_hbm)]
    for load in loads:
        load.start()
    pairs = nz // 2
    bits = nz.bit_length() - 1
    feat = ew.shape[0]
    fpad = xs.shape[2]
    wl = o_dw.shape[1]
    win_w = nz * wl
    rowx = pairs * CAP
    dp = lax.axis_index("dp")
    ex = lax.axis_index("expert")
    core = lax.axis_index("tensor")
    x, z = ex // nz, ex % nz
    zh, y = dp // ny, dp % ny
    pair, par = z // 2, z % 2

    def at_x(d):
        return (dp, lax.rem(x + d, nx) * nz + z, core)

    def at_z(zz):
        return (dp, x * nz + zz, core)

    beside = at_z(z + 1 - 2 * par)
    other_core = (dp, ex, 1 - core)

    def at_y(d):
        return (zh * ny + lax.rem(y + d, ny), ex, core)

    other_h = ((1 - zh) * ny + y, ex, core)

    def copy(src, dst, send, recv, dev):
        return pltpu.make_async_remote_copy(
            src_ref=src, dst_ref=dst, send_sem=send, recv_sem=recv,
            device_id=dev, device_id_type=MESH,
        )

    blk = nx * CAP
    higher_z, higher_beside, higher_h = in_sem.at[1], in_sem.at[0], in_sem.at[2]

    def signal(sem, dev):
        pl.semaphore_signal(sem, inc=1, device_id=dev, device_id_type=MESH)

    def at_ring(d):
        around = zh * pairs + pair + d - pairs * goes_back(d)
        around = lax.rem(around + nh * pairs, nh * pairs)
        first = lax.rem(around, pairs) * 2 + goes_back(d)
        return ((around // pairs) * ny + y, x * nz + first, core)

    def goes_back(d):
        return (2 * d + core) // (pairs + 1)

    def far_first(i):
        return pairs // 2 + (i // 2) * (1 - 2 * (i % 2))

    def at_other_h(zz):
        return ((1 - zh) * ny + y, x * nz + zz, core)

    same_z = [at_x(d) for d in range(1, nx)] + [other_core] + [at_y(d) for d in range(1, ny)]
    barrier = pltpu.get_barrier_semaphore()
    for dev in same_z:
        signal(barrier, dev)

    @pl.when(par == 0)
    def _():
        signal(barrier, beside)

    @pl.loop(0, nz)
    def _(zz):
        @pl.when(zz // 2 > pair)
        def _():
            signal(barrier, at_z(zz))

        @pl.when(zh == 0)
        def _():
            signal(barrier, at_other_h(zz))

    pl.semaphore_wait(barrier, len(same_z) + 2 * pair + par + zh * nz)

    @pl.when(par == 1)
    def _():
        signal(higher_beside, beside)

    @pl.loop(0, nz)
    def _(zz):
        @pl.when(zz // 2 < pair)
        def _():
            signal(higher_z, at_z(zz))

        @pl.when(zh == 1)
        def _():
            signal(higher_h, at_other_h(zz))

    r = rt[...]
    e_row = lax.broadcasted_iota(jnp.int32, (e_mat.shape[1], r.shape[1]), 0)
    member = ((e_row == r[0:1, :]) | (e_row == r[1:2, :])).astype(F32).astype(BF16)
    n_tok = r.shape[1]
    before = lax.broadcasted_iota(jnp.int32, (n_tok, n_tok), 0) < lax.broadcasted_iota(
        jnp.int32, (n_tok, n_tok), 1
    )
    rank = dot(member, before.astype(F32).astype(BF16), 1, 0).astype(BF16)
    is_member = dot(e_mat[...], member, 1, 0)
    ranks = dot(e_mat[...], rank, 1, 0)
    dmat[...] = ((is_member > 0.5) & (ranks == m_mat[...])).astype(F32).astype(BF16)
    chip_w = 2 * feat
    pick_r = lax.broadcasted_iota(jnp.int32, (chip_w, fpad), 0)
    pick_c = lax.broadcasted_iota(jnp.int32, (chip_w, fpad), 1)
    pick = ((pick_r == pick_c + core * feat) & (pick_c < feat)).astype(F32).astype(BF16)

    def features(group):
        window = li[:, pl.ds(pl.multiple_of(group * chip_w, 128), chip_w)]
        return dot(window, pick, 1, 0).astype(BF16)

    mine, theirs = features(dp), features((1 - zh) * ny + y)
    row = lax.broadcasted_iota(jnp.int32, (rowx, fpad), 0)
    to_pair = sum((row >= k * CAP).astype(jnp.int32) for k in range(1, pairs))
    dist = to_pair - pair + jnp.where(to_pair < pair, pairs, 0)
    back = (dist > pairs // 2) | ((dist == pairs // 2) & (core == 1))
    crosses = pair + dist - jnp.where(back, pairs, 0) != to_pair
    for i in range(nx):
        rows_i = dmat[i * rowx:(i + 1) * rowx, :]
        xs[i] = jnp.where(crosses, dot(rows_i, theirs, 1, 0), dot(rows_i, mine, 1, 0)).astype(BF16)
    xr[x] = xs[x]

    def dx_copy(d, slot):
        return copy(xs.at[lax.rem(x + d, nx)], xr.at[slot], dx_s.at[d], dx_r.at[d], at_x(d))

    for d in range(1, nx):
        dx_copy(d, x).start()

    for load in loads[:3]:
        load.wait()
    rows_t = ecot.shape[0] // 4
    @pl.loop(0, 4)
    def _(i):
        at = pl.ds(pl.multiple_of(i * rows_t, 16), rows_t)
        prt[at, :] = dot(ecot[at, :], ew[...], 1, 1).astype(BF16)

    for i in range(2):
        half = p_z[i * pairs * blk:(i + 1) * pairs * blk, :]
        pz[i] = pack(dot(half, prt[...], 1, 0), blk, feat).astype(BF16)

    def pe_copy(sp, k):
        i = 2 * k + sp
        return copy(pz.at[sp, k], pin.at[sp, k], pe_s.at[i], pe_r.at[i], beside)

    def on_side(side, k):
        return (k - pair) * (2 * side - 1) > 0

    def each_on(side, fn):
        @pl.loop(0, pairs)
        def _(i):
            k = i + side * (pairs - 1 - 2 * i)

            @pl.when(on_side(side, k))
            def _():
                fn(0, k)
                fn(1, k)

    @pl.when(par == 0)
    def _():
        pl.semaphore_wait(higher_beside, 1)

    each_on(1 - par, lambda sp, k: pe_copy(sp, k).start())
    pe_copy(1 - par, pair).start()

    for d in range(1, nx):
        dx_copy(d, lax.rem(x + nx - d, nx)).wait_recv()
    sorted_rows = dot(p_x[...], xr[...].reshape(nx * rowx, fpad), 1, 0)
    zs[...] = pack(sorted_rows, blk, feat).astype(BF16)

    def dz_copy(d, side, slot):
        return copy(
            zs.at[lax.rem(pair + d, pairs)], zr.at[side, slot],
            dz_s.at[d], dz_r.at[2 * d + side], at_ring(d),
        )

    def df_copy(d, side):
        slot = lax.rem(pair + pairs - d, pairs)
        i = 2 * d + side
        return copy(zr.at[side, slot], zr.at[side, slot], df_s.at[i], df_r.at[i], beside)

    def each_way(back, fn):
        @pl.loop(1, pairs)
        def _(i):
            d = far_first(i)

            @pl.when(goes_back(d) == back)
            def _():
                fn(d, 0)
                fn(d, 1)

    zr[par, pair] = zs[pair]
    df_copy(0, par).start()

    def send_rows(same_h):
        @pl.loop(1, pairs)
        def _(i):
            d = far_first(i)

            @pl.when((at_ring(d)[0] == dp) == same_h)
            def _():
                dz_copy(d, par, pair).start()

    def wait_higher_z():
        @pl.when(pair < pairs - 1)
        def _():
            pl.semaphore_wait(higher_z, 2 * (pairs - 1 - pair))

    @pl.when(zh == 1)
    def _():
        wait_higher_z()
        send_rows(True)
        send_rows(False)

    loads[3].wait()

    def c_copy(k):
        return copy(dsend.at[k], dcore.at[k], c_s.at[k], c_r.at[k], other_core)

    @pl.loop(0, nh * ny)
    def _(k):
        part = dot(wt[:, pl.ds(pl.multiple_of(k * chip_w, 128), chip_w)], cot[...], 0, 0)
        low, high = part[0:feat, :], part[feat:, :]
        dacc[k] = jnp.where(core == 0, low, high)
        dsend[k] = jnp.where(core == 0, high, low).astype(BF16)
        c_copy(k).start()

    def wx_copy(d):
        return copy(wxs.at[d - 1], wxr.at[d - 1], wx_s.at[d], wx_r.at[d], at_x(d))

    def wblock(xx):
        w_in = li[:, pl.ds(pl.multiple_of(xx * win_w, 128), win_w)]
        return dot(cot[...], w_in, 1, 0)

    for d in range(1, nx):
        got = wblock(lax.rem(x + d, nx))
        for q in range(nz):
            wxs[d - 1, rev_bits(q, bits), :, 0:wl] = got[:, q * wl:(q + 1) * wl].astype(BF16)
        wxs[d - 1, :, :, wl:] = jnp.zeros((nz, wxs.shape[2], wxs.shape[3] - wl), BF16)
        wx_copy(d).start()
    got = wblock(x)
    for q in range(nz):
        wz[rev_bits(q, bits), :, 0:wl] = got[:, q * wl:(q + 1) * wl]
    wz[:, :, wl:] = jnp.zeros((nz, wz.shape[1], wz.shape[2] - wl), F32)

    def y_copy(d):
        return copy(ysend.at[d - 1], yrecv.at[d - 1], y_s.at[d], y_r.at[d], at_y(d))

    def core_sum(k):
        c_copy(k).wait_recv()
        return dacc[k] + dcore[k].astype(F32)

    for d in range(1, ny):
        for h in range(nh):
            ysend[d - 1, h] = core_sum(h * ny + lax.rem(y + d, ny)).astype(BF16)
        y_copy(d).start()
    for h in range(nh):
        dacc[h * ny + y] = core_sum(h * ny + y)

    @pl.when(zh == 0)
    def _():
        wait_higher_z()
        send_rows(True)

    def rz_copy(sp, k, slot):
        return copy(rs.at[sp, k], rz.at[slot], rz_s.at[2 * k + sp], rz_r.at[slot], at_z(2 * k + sp))

    def pair_sum(sp, k):
        pe_copy(sp, k).wait_recv()
        return (pz[sp, k].astype(F32) + pin[sp, k].astype(F32)).astype(BF16)

    def return_rows(sp, k):
        rs[sp, k] = pair_sum(sp, k)
        rz_copy(sp, k, pair).start()

    each_on(par, return_rows)
    rz[pair] = pair_sum(par, pair)

    @pl.when(zh == 0)
    def _():
        pl.semaphore_wait(higher_h, nz)
        send_rows(False)

    def h_copy():
        return copy(hsend, hrecv, h_s.at[0], h_r.at[0], other_h)

    for d in range(1, ny):
        y_copy(d).wait_recv()
    for h in range(nh):
        total = dacc[h * ny + y]
        for d in range(1, ny):
            total = total + yrecv[d - 1, h].astype(F32)
        dacc[h * ny + y] = total
    hsend[...] = dacc[(1 - zh) * ny + y].astype(BF16)

    h_copy().start()

    def wz_at(step):
        base, size = 0, nz
        for b in range(step):
            size = size // 2
            base = base + ((z // (1 << b)) % 2) * size
        return base, size

    def wz_copy(step):
        size = nz >> (step + 1)
        at = pl.ds(nz - 2 * size, size)
        bit = (z // (1 << step)) % 2
        partner = at_z(z + (1 - 2 * bit) * (1 << step))
        return copy(wzs.at[at], wzr.at[at], wz_s.at[step], wz_r.at[step], partner)

    def wz_step(step, total):
        base, size = wz_at(step)
        if step < bits:
            size = size // 2
            bit = (z // (1 << step)) % 2
            away, base = base + (1 - bit) * size, base + bit * size

            @pl.loop(0, size)
            def _(i):
                wzs[nz - 2 * size + i] = total(away + i).astype(BF16)

            wz_copy(step).start()

        @pl.loop(0, size)
        def _(i):
            wz[base + i] = total(base + i)

    def wz_next(step):
        wz_copy(step - 1).wait_recv()
        base, size = wz_at(step)
        land = nz - 2 * size
        wz_step(step, lambda i: wz[i] + wzr[land + i - base].astype(F32))

    for d in range(1, nx):
        wx_copy(d).wait_recv()

    def over_x(i):
        total = wz[i]
        for d in range(1, nx):
            total = total + wxr[d - 1, i].astype(F32)
        return total

    wz_step(0, over_x)

    def forward(d, side):
        dz_copy(d, side, lax.rem(pair + pairs - d, pairs)).wait_recv()
        df_copy(d, side).start()

    each_way(par, forward)

    wz_next(1)

    @pl.loop(0, pairs)
    def _(k):
        @pl.when(k != pair)
        def _():
            rz_copy(par, k, k).wait_recv()

    back_rows = dot(p_x[...], unpack(rz[...], blk, feat), 0, 0).astype(BF16)
    qs[:, :, 0:feat] = back_rows.reshape(nx, rowx, feat)
    qs[:, :, feat:] = jnp.zeros((nx, rowx, fpad - feat), BF16)

    def rx_copy(d, slot):
        return copy(qs.at[lax.rem(x + d, nx)], rx.at[slot], rx_s.at[d], rx_r.at[d], at_x(d))

    for d in range(1, nx):
        rx_copy(d, x).start()
    rx[x] = qs[x]

    if bits > 2:
        wz_next(2)

    each_way(1 - par, lambda d, side: df_copy(d, side).wait_recv())
    df_copy(0, 1 - par).wait_recv()

    for i in range(2):
        half = p_z[i * pairs * blk:(i + 1) * pairs * blk, :]
        part = dot(half, unpack(zr[i], blk, feat), 0, 0)
        if i == 0:
            ordered = part
        else:
            ordered = ordered + part
    prt[...] = ordered.astype(BF16)
    cols = 256

    @pl.loop(0, ecot.shape[1] // cols)
    def _(i):
        at = pl.ds(pl.multiple_of(i * cols, 128), cols)
        o_ew[:, at] = dot(prt[...], ecot[:, at], 0, 0).astype(BF16)

    for step in range(min(3, bits), bits + 1):
        wz_next(step)
    base, _ = wz_at(bits)
    o_dw[...] = wz[base][:, 0:wl]

    h_copy().wait_recv()
    for d in range(1, nx):
        rx_copy(d, lax.rem(x + nx - d, nx)).wait_recv()
    expert_sum = dot(rx[...].reshape(nx * rowx, fpad), dmat[...], 0, 0)[0:feat, :]
    dense_sum = dacc[zh * ny + y] + hrecv[...].astype(F32)
    o_in[...] = (expert_sum + dense_sum).astype(BF16)

    for d in range(1, nx):
        dx_copy(d, x).wait_send()
        rx_copy(d, x).wait_send()
        wx_copy(d).wait_send()
    for d in range(1, ny):
        y_copy(d).wait_send()
    h_copy().wait_send()
    for step in range(bits):
        wz_copy(step).wait_send()

    @pl.loop(1, pairs)
    def _(d):
        dz_copy(d, par, pair).wait_send()

    each_way(par, lambda d, side: df_copy(d, side).wait_send())
    df_copy(0, par).wait_send()
    each_on(1 - par, lambda sp, k: pe_copy(sp, k).wait_send())
    pe_copy(1 - par, pair).wait_send()
    each_on(par, lambda sp, k: rz_copy(sp, k, pair).wait_send())

    @pl.loop(0, nh * ny)
    def _(k):
        c_copy(k).wait_send()


def body(nx, ny, layer_input, routes, dense_cot, dense_weight, expert_cot, expert_weight):
    nz = lax.axis_size("expert") // nx
    nh = lax.axis_size("dp") // ny
    pairs = nz // 2
    bits = nz.bit_length() - 1
    experts = nx * pairs
    tok, width = layer_input.shape
    feat, cols = expert_weight.shape
    hid = dense_cot.shape[1]
    slots = experts * CAP
    rows = 2 * slots
    fpad = up(feat, 128)
    wl = width // (nx * nz)
    wpad = up(wl, 128)
    rowx, blk = pairs * CAP, nx * CAP
    prows = packed_rows(blk, feat)

    px = np.zeros((slots, slots), np.float32)
    for p in range(pairs):
        for s in range(nx):
            for c in range(CAP):
                px[p * blk + s * CAP + c, s * rowx + p * CAP + c] = 1
    pz = np.zeros((rows, rows), np.float32)
    for q in range(nz):
        for s in range(nx):
            for c in range(CAP):
                pz[(q % 2) * slots + (q // 2) * blk + s * CAP + c, (s * nz + q) * CAP + c] = 1
    slot = np.arange(slots)
    e_mat = (slot[:, None] // CAP == np.arange(experts)[None, :]).astype(np.float32)
    m_mat = np.broadcast_to((slot % CAP)[:, None], (slots, tok)).astype(np.float32)

    dma = pltpu.SemaphoreType.DMA
    vm = pltpu.VMEM
    groups = nh * ny
    scratch = [
        vm((slots, tok), BF16),
        vm((nx, rowx, fpad), BF16), vm((nx, rowx, fpad), BF16),
        vm((pairs, prows, 128), BF16), vm((2, pairs, prows, 128), BF16),
        vm((rows, feat), BF16), vm((2, pairs, prows, 128), BF16), vm((2, pairs, prows, 128), BF16),
        vm((2, pairs, prows, 128), BF16), vm((pairs, prows, 128), BF16),
        vm((nx, rowx, fpad), BF16), vm((nx, rowx, fpad), BF16),
        vm((groups, feat, tok), F32), vm((groups, feat, tok), BF16), vm((groups, feat, tok), BF16),
        vm((ny - 1, nh, feat, tok), BF16), vm((ny - 1, nh, feat, tok), BF16),
        vm((feat, tok), BF16), vm((feat, tok), BF16),
        vm((nx - 1, nz, hid, wpad), BF16), vm((nx - 1, nz, hid, wpad), BF16),
        vm((nz, hid, wpad), F32), vm((nz, hid, wpad), BF16), vm((nz, hid, wpad), BF16),
        pltpu.SemaphoreType.REGULAR((3,)),
        vm((hid, width), BF16), vm((rows, cols), BF16), vm((feat, cols), BF16),
        vm((rows, rows), BF16), dma((4,)),
    ]
    for count in (nx, nz, nz, nz, nz, nx, groups, ny, 1, nx, bits):
        scratch += [dma((count,)), dma((count,))]
    full = pl.BlockSpec(memory_space=pltpu.VMEM)
    hbm = pl.BlockSpec(memory_space=pl.ANY)
    in_t, dw_t, ew_out = pl.pallas_call(
        functools.partial(kernel, (nx, nz, ny, nh)),
        out_shape=(
            jax.ShapeDtypeStruct((feat, tok), BF16),
            jax.ShapeDtypeStruct((hid, wl), F32),
            jax.ShapeDtypeStruct((feat, cols), BF16),
        ),
        in_specs=[full] * 3 + [hbm] * 3 + [full, hbm, full, full],
        out_specs=(full, full, full),
        scratch_shapes=scratch,
        compiler_params=pltpu.CompilerParams(
            collective_id=0, has_side_effects=True, vmem_limit_bytes=56 * 1024 * 1024
        ),
    )(
        layer_input, routes.T, dense_cot.T, dense_weight.T, expert_cot, expert_weight,
        jnp.asarray(px, BF16), jnp.asarray(pz, BF16), jnp.asarray(e_mat, BF16),
        jnp.asarray(m_mat, F32),
    )
    return (in_t.T, dw_t.T, ew_out)


def solution(mesh, nx=NX, ny=NY):
    placed = (
        P("expert", None),
        P("expert", None),
        P("expert", ("dp", "tensor")),
        P(None, ("dp", "tensor")),
        P(None, "expert"),
        P(("dp", "tensor"), "expert"),
    )
    return jax.shard_map(
        functools.partial(body, nx, ny),
        mesh=mesh,
        in_specs=placed,
        out_specs=(
            P("expert", ("dp", "tensor")),
            P("expert", ("dp", "tensor")),
            P(("dp", "tensor"), "expert"),
        ),
        check_vma=False,
    )
```

```python
import functools

import jax
import jax.numpy as jnp
import numpy as np
from jax import lax
from jax.experimental import pallas as pl
from jax.experimental.pallas import tpu as pltpu
from jax.sharding import PartitionSpec as P

MESH = pl.DeviceIdType.MESH
F32 = jnp.float32
BF16 = jnp.bfloat16
CAP = 12
NX, NY = 4, 4


def dot(a, b, ca, cb):
    return lax.dot_general(a, b, (((ca,), (cb,)), ((), ())), preferred_element_type=F32)


def rev_bits(q, bits):
    return sum(((q >> b) & 1) << (bits - 1 - b) for b in range(bits))


def up(n, m):
    return -(-n // m) * m


def pack(v, blk, feat):
    n = v.shape[0] // blk
    whole, rest = feat // 128, feat % 128
    v = v.reshape(n, blk, v.shape[1])
    parts = [v[:, :, t * 128:(t + 1) * 128] for t in range(whole)]
    if rest:
        half = blk // 2
        last = v[:, :, whole * 128:feat]
        parts.append(jnp.concatenate([last[:, :half, :], last[:, half:, :]], axis=2))
        parts.append(jnp.zeros((n, packed_rows(blk, feat) - whole * blk - half, 128), v.dtype))
    return jnp.concatenate(parts, axis=1)


def unpack(v, blk, feat):
    n = v.shape[0]
    whole, rest = feat // 128, feat % 128
    parts = [v[:, t * blk:(t + 1) * blk, :].reshape(n * blk, 128) for t in range(whole)]
    if rest:
        half = blk // 2
        last = v[:, whole * blk:, :].astype(F32)
        last = jnp.concatenate([last[:, :half, :rest], last[:, :half, rest:]], axis=1)
        parts.append(last.reshape(n * blk, rest).astype(v.dtype))
    return jnp.concatenate(parts, axis=1) if len(parts) > 1 else parts[0]


def packed_rows(blk, feat):
    return feat // 128 * blk + (up(blk // 2, 16) if feat % 128 else 0)


def kernel(
    dims,
    li, rt, cot, wt_hbm, ecot_hbm, ew_hbm, p_x, p_z_hbm, e_mat, m_mat,
    o_in, o_dw, o_ew,
    dmat, xs, xr, zs, zr, prt, pz, pin, rs, rz, qs, rx,
    dacc, dsend, dcore, ysend, yrecv, hsend, hrecv,
    wxs, wxr, wz, wzs, wzr, in_sem, wt, ecot, ew, p_z, load_s,
    dx_s, dx_r, dz_s, dz_r, df_s, df_r, pe_s, pe_r, rz_s, rz_r, rx_s, rx_r,
    c_s, c_r, y_s, y_r, h_s, h_r, wx_s, wx_r, wz_s, wz_r,
):
    nx, nz, ny, nh = dims
    from_hbm = ((ecot_hbm, ecot), (ew_hbm, ew), (p_z_hbm, p_z), (wt_hbm, wt))
    loads = [pltpu.make_async_copy(a, b, load_s.at[i]) for i, (a, b) in enumerate(from_hbm)]
    for load in loads:
        load.start()
    pairs = nz // 2
    bits = nz.bit_length() - 1
    feat = ew.shape[0]
    fpad = xs.shape[2]
    wl = o_dw.shape[1]
    win_w = nz * wl
    rowx = pairs * CAP
    dp = lax.axis_index("dp")
    ex = lax.axis_index("expert")
    core = lax.axis_index("tensor")
    x, z = ex // nz, ex % nz
    zh, y = dp // ny, dp % ny
    pair, par = z // 2, z % 2

    def at_x(d):
        return (dp, lax.rem(x + d, nx) * nz + z, core)

    def at_z(zz):
        return (dp, x * nz + zz, core)

    beside = at_z(z + 1 - 2 * par)
    other_core = (dp, ex, 1 - core)

    def at_y(d):
        return (zh * ny + lax.rem(y + d, ny), ex, core)

    other_h = ((1 - zh) * ny + y, ex, core)

    def copy(src, dst, send, recv, dev):
        return pltpu.make_async_remote_copy(
            src_ref=src, dst_ref=dst, send_sem=send, recv_sem=recv,
            device_id=dev, device_id_type=MESH,
        )

    blk = nx * CAP
    higher_z, higher_beside, higher_h = in_sem.at[1], in_sem.at[0], in_sem.at[2]

    def signal(sem, dev):
        pl.semaphore_signal(sem, inc=1, device_id=dev, device_id_type=MESH)

    def at_ring(d):
        around = zh * pairs + pair + d - pairs * goes_back(d)
        around = lax.rem(around + nh * pairs, nh * pairs)
        first = lax.rem(around, pairs) * 2 + goes_back(d)
        return ((around // pairs) * ny + y, x * nz + first, core)

    def goes_back(d):
        return (2 * d + core) // (pairs + 1)

    def far_first(i):
        return pairs // 2 + (i // 2) * (1 - 2 * (i % 2))

    def at_other_h(zz):
        return ((1 - zh) * ny + y, x * nz + zz, core)

    same_z = [at_x(d) for d in range(1, nx)] + [other_core] + [at_y(d) for d in range(1, ny)]
    barrier = pltpu.get_barrier_semaphore()
    for dev in same_z:
        signal(barrier, dev)

    @pl.when(par == 0)
    def _():
        signal(barrier, beside)

    @pl.loop(0, nz)
    def _(zz):
        @pl.when(zz // 2 > pair)
        def _():
            signal(barrier, at_z(zz))

        @pl.when(zh == 0)
        def _():
            signal(barrier, at_other_h(zz))

    pl.semaphore_wait(barrier, len(same_z) + 2 * pair + par + zh * nz)

    @pl.when(par == 1)
    def _():
        signal(higher_beside, beside)

    @pl.loop(0, nz)
    def _(zz):
        @pl.when(zz // 2 < pair)
        def _():
            signal(higher_z, at_z(zz))

        @pl.when(zh == 1)
        def _():
            signal(higher_h, at_other_h(zz))

    r = rt[...]
    e_row = lax.broadcasted_iota(jnp.int32, (e_mat.shape[1], r.shape[1]), 0)
    member = ((e_row == r[0:1, :]) | (e_row == r[1:2, :])).astype(F32).astype(BF16)
    n_tok = r.shape[1]
    before = lax.broadcasted_iota(jnp.int32, (n_tok, n_tok), 0) < lax.broadcasted_iota(
        jnp.int32, (n_tok, n_tok), 1
    )
    rank = dot(member, before.astype(F32).astype(BF16), 1, 0).astype(BF16)
    is_member = dot(e_mat[...], member, 1, 0)
    ranks = dot(e_mat[...], rank, 1, 0)
    dmat[...] = ((is_member > 0.5) & (ranks == m_mat[...])).astype(F32).astype(BF16)
    chip_w = 2 * feat
    pick_r = lax.broadcasted_iota(jnp.int32, (chip_w, fpad), 0)
    pick_c = lax.broadcasted_iota(jnp.int32, (chip_w, fpad), 1)
    pick = ((pick_r == pick_c + core * feat) & (pick_c < feat)).astype(F32).astype(BF16)

    def features(group):
        window = li[:, pl.ds(pl.multiple_of(group * chip_w, 128), chip_w)]
        return dot(window, pick, 1, 0).astype(BF16)

    mine, theirs = features(dp), features((1 - zh) * ny + y)
    row = lax.broadcasted_iota(jnp.int32, (rowx, fpad), 0)
    to_pair = sum((row >= k * CAP).astype(jnp.int32) for k in range(1, pairs))
    dist = to_pair - pair + jnp.where(to_pair < pair, pairs, 0)
    back = (dist > pairs // 2) | ((dist == pairs // 2) & (core == 1))
    crosses = pair + dist - jnp.where(back, pairs, 0) != to_pair
    for i in range(nx):
        rows_i = dmat[i * rowx:(i + 1) * rowx, :]
        xs[i] = jnp.where(crosses, dot(rows_i, theirs, 1, 0), dot(rows_i, mine, 1, 0)).astype(BF16)
    xr[x] = xs[x]

    def dx_copy(d, slot):
        return copy(xs.at[lax.rem(x + d, nx)], xr.at[slot], dx_s.at[d], dx_r.at[d], at_x(d))

    for d in range(1, nx):
        dx_copy(d, x).start()

    for load in loads[:3]:
        load.wait()
    rows_t = ecot.shape[0] // 4
    @pl.loop(0, 4)
    def _(i):
        at = pl.ds(pl.multiple_of(i * rows_t, 16), rows_t)
        prt[at, :] = dot(ecot[at, :], ew[...], 1, 1).astype(BF16)

    for i in range(2):
        half = p_z[i * pairs * blk:(i + 1) * pairs * blk, :]
        pz[i] = pack(dot(half, prt[...], 1, 0), blk, feat).astype(BF16)

    def pe_copy(sp, k):
        i = 2 * k + sp
        return copy(pz.at[sp, k], pin.at[sp, k], pe_s.at[i], pe_r.at[i], beside)

    def on_side(side, k):
        return (k - pair) * (2 * side - 1) > 0

    def each_on(side, fn):
        @pl.loop(0, pairs)
        def _(i):
            k = i + side * (pairs - 1 - 2 * i)

            @pl.when(on_side(side, k))
            def _():
                fn(0, k)
                fn(1, k)

    @pl.when(par == 0)
    def _():
        pl.semaphore_wait(higher_beside, 1)

    each_on(1 - par, lambda sp, k: pe_copy(sp, k).start())
    pe_copy(1 - par, pair).start()

    for d in range(1, nx):
        dx_copy(d, lax.rem(x + nx - d, nx)).wait_recv()
    sorted_rows = dot(p_x[...], xr[...].reshape(nx * rowx, fpad), 1, 0)
    zs[...] = pack(sorted_rows, blk, feat).astype(BF16)

    def dz_copy(d, side, slot):
        return copy(
            zs.at[lax.rem(pair + d, pairs)], zr.at[side, slot],
            dz_s.at[d], dz_r.at[2 * d + side], at_ring(d),
        )

    def df_copy(d, side):
        slot = lax.rem(pair + pairs - d, pairs)
        i = 2 * d + side
        return copy(zr.at[side, slot], zr.at[side, slot], df_s.at[i], df_r.at[i], beside)

    def each_way(back, fn):
        @pl.loop(1, pairs)
        def _(i):
            d = pairs * (1 - i % 2) + (2 * (i % 2) - 1) * ((i + 1) // 2)

            @pl.when(goes_back(d) == back)
            def _():
                fn(d, 0)
                fn(d, 1)

    zr[par, pair] = zs[pair]
    df_copy(0, par).start()

    def send_rows(same_h):
        @pl.loop(1, pairs)
        def _(i):
            d = far_first(i)

            @pl.when((at_ring(d)[0] == dp) == same_h)
            def _():
                dz_copy(d, par, pair).start()

    def wait_higher_z():
        @pl.when(pair < pairs - 1)
        def _():
            pl.semaphore_wait(higher_z, 2 * (pairs - 1 - pair))

    @pl.when(zh == 1)
    def _():
        wait_higher_z()
        send_rows(True)
        send_rows(False)

    loads[3].wait()

    def c_copy(k):
        return copy(dsend.at[k], dcore.at[k], c_s.at[k], c_r.at[k], other_core)

    @pl.loop(0, nh * ny)
    def _(k):
        part = dot(wt[:, pl.ds(pl.multiple_of(k * chip_w, 128), chip_w)], cot[...], 0, 0)
        low, high = part[0:feat, :], part[feat:, :]
        dacc[k] = jnp.where(core == 0, low, high)
        dsend[k] = jnp.where(core == 0, high, low).astype(BF16)
        c_copy(k).start()

    def wx_copy(d):
        return copy(wxs.at[d - 1], wxr.at[d - 1], wx_s.at[d], wx_r.at[d], at_x(d))

    def wblock(xx):
        w_in = li[:, pl.ds(pl.multiple_of(xx * win_w, 128), win_w)]
        return dot(cot[...], w_in, 1, 0)

    for d in range(1, nx):
        got = wblock(lax.rem(x + d, nx))
        for q in range(nz):
            wxs[d - 1, rev_bits(q, bits), :, 0:wl] = got[:, q * wl:(q + 1) * wl].astype(BF16)
        wxs[d - 1, :, :, wl:] = jnp.zeros((nz, wxs.shape[2], wxs.shape[3] - wl), BF16)
        wx_copy(d).start()
    got = wblock(x)
    for q in range(nz):
        wz[rev_bits(q, bits), :, 0:wl] = got[:, q * wl:(q + 1) * wl]
    wz[:, :, wl:] = jnp.zeros((nz, wz.shape[1], wz.shape[2] - wl), F32)

    def y_copy(d):
        return copy(ysend.at[d - 1], yrecv.at[d - 1], y_s.at[d], y_r.at[d], at_y(d))

    def core_sum(k):
        c_copy(k).wait_recv()
        return dacc[k] + dcore[k].astype(F32)

    for d in range(1, ny):
        for h in range(nh):
            ysend[d - 1, h] = core_sum(h * ny + lax.rem(y + d, ny)).astype(BF16)
        y_copy(d).start()
    for h in range(nh):
        dacc[h * ny + y] = core_sum(h * ny + y)

    def h_copy():
        return copy(hsend, hrecv, h_s.at[0], h_r.at[0], other_h)

    for d in range(1, ny):
        y_copy(d).wait_recv()
    for h in range(nh):
        total = dacc[h * ny + y]
        for d in range(1, ny):
            total = total + yrecv[d - 1, h].astype(F32)
        dacc[h * ny + y] = total
    hsend[...] = dacc[(1 - zh) * ny + y].astype(BF16)

    @pl.when(zh == 1)
    def _():
        h_copy().start()

    @pl.when(zh == 0)
    def _():
        wait_higher_z()
        send_rows(True)

    def rz_copy(sp, k, slot):
        return copy(rs.at[sp, k], rz.at[slot], rz_s.at[2 * k + sp], rz_r.at[slot], at_z(2 * k + sp))

    def pair_sum(sp, k):
        pe_copy(sp, k).wait_recv()
        return (pz[sp, k].astype(F32) + pin[sp, k].astype(F32)).astype(BF16)

    def return_rows(sp, k):
        rs[sp, k] = pair_sum(sp, k)
        rz_copy(sp, k, pair).start()

    each_on(par, return_rows)
    rz[pair] = pair_sum(par, pair)

    @pl.when(zh == 0)
    def _():
        pl.semaphore_wait(higher_h, nz)
        h_copy().start()
        send_rows(False)

    def wz_at(step):
        base, size = 0, nz
        for b in range(step):
            size = size // 2
            base = base + ((z // (1 << b)) % 2) * size
        return base, size

    def wz_copy(step):
        size = nz >> (step + 1)
        at = pl.ds(nz - 2 * size, size)
        bit = (z // (1 << step)) % 2
        partner = at_z(z + (1 - 2 * bit) * (1 << step))
        return copy(wzs.at[at], wzr.at[at], wz_s.at[step], wz_r.at[step], partner)

    def wz_step(step, total):
        base, size = wz_at(step)
        if step < bits:
            size = size // 2
            bit = (z // (1 << step)) % 2
            away, base = base + (1 - bit) * size, base + bit * size

            @pl.loop(0, size)
            def _(i):
                wzs[nz - 2 * size + i] = total(away + i).astype(BF16)

            wz_copy(step).start()

        @pl.loop(0, size)
        def _(i):
            wz[base + i] = total(base + i)

    def wz_next(step):
        wz_copy(step - 1).wait_recv()
        base, size = wz_at(step)
        land = nz - 2 * size
        wz_step(step, lambda i: wz[i] + wzr[land + i - base].astype(F32))

    for d in range(1, nx):
        wx_copy(d).wait_recv()

    def over_x(i):
        total = wz[i]
        for d in range(1, nx):
            total = total + wxr[d - 1, i].astype(F32)
        return total

    wz_step(0, over_x)

    def forward(d, side):
        dz_copy(d, side, lax.rem(pair + pairs - d, pairs)).wait_recv()
        df_copy(d, side).start()

    each_way(par, forward)

    wz_next(1)

    @pl.loop(0, pairs)
    def _(k):
        @pl.when(k != pair)
        def _():
            rz_copy(par, k, k).wait_recv()

    back_rows = dot(p_x[...], unpack(rz[...], blk, feat), 0, 0).astype(BF16)
    qs[:, :, 0:feat] = back_rows.reshape(nx, rowx, feat)
    qs[:, :, feat:] = jnp.zeros((nx, rowx, fpad - feat), BF16)

    def rx_copy(d, slot):
        return copy(qs.at[lax.rem(x + d, nx)], rx.at[slot], rx_s.at[d], rx_r.at[d], at_x(d))

    for d in range(1, nx):
        rx_copy(d, x).start()
    rx[x] = qs[x]

    if bits > 2:
        wz_next(2)

    each_way(1 - par, lambda d, side: df_copy(d, side).wait_recv())
    df_copy(0, 1 - par).wait_recv()

    for i in range(2):
        half = p_z[i * pairs * blk:(i + 1) * pairs * blk, :]
        part = dot(half, unpack(zr[i], blk, feat), 0, 0)
        if i == 0:
            ordered = part
        else:
            ordered = ordered + part
    prt[...] = ordered.astype(BF16)
    cols = 256

    @pl.loop(0, ecot.shape[1] // cols)
    def _(i):
        at = pl.ds(pl.multiple_of(i * cols, 128), cols)
        o_ew[:, at] = dot(prt[...], ecot[:, at], 0, 0).astype(BF16)

    for step in range(min(3, bits), bits + 1):
        wz_next(step)
    base, _ = wz_at(bits)
    o_dw[...] = wz[base][:, 0:wl]

    h_copy().wait_recv()
    for d in range(1, nx):
        rx_copy(d, lax.rem(x + nx - d, nx)).wait_recv()
    expert_sum = dot(rx[...].reshape(nx * rowx, fpad), dmat[...], 0, 0)[0:feat, :]
    dense_sum = dacc[zh * ny + y] + hrecv[...].astype(F32)
    o_in[...] = (expert_sum + dense_sum).astype(BF16)

    for d in range(1, nx):
        dx_copy(d, x).wait_send()
        rx_copy(d, x).wait_send()
        wx_copy(d).wait_send()
    for d in range(1, ny):
        y_copy(d).wait_send()
    h_copy().wait_send()
    for step in range(bits):
        wz_copy(step).wait_send()

    @pl.loop(1, pairs)
    def _(d):
        dz_copy(d, par, pair).wait_send()

    each_way(par, lambda d, side: df_copy(d, side).wait_send())
    df_copy(0, par).wait_send()
    each_on(1 - par, lambda sp, k: pe_copy(sp, k).wait_send())
    pe_copy(1 - par, pair).wait_send()
    each_on(par, lambda sp, k: rz_copy(sp, k, pair).wait_send())

    @pl.loop(0, nh * ny)
    def _(k):
        c_copy(k).wait_send()


def body(nx, ny, layer_input, routes, dense_cot, dense_weight, expert_cot, expert_weight):
    nz = lax.axis_size("expert") // nx
    nh = lax.axis_size("dp") // ny
    pairs = nz // 2
    bits = nz.bit_length() - 1
    experts = nx * pairs
    tok, width = layer_input.shape
    feat, cols = expert_weight.shape
    hid = dense_cot.shape[1]
    slots = experts * CAP
    rows = 2 * slots
    fpad = up(feat, 128)
    wl = width // (nx * nz)
    wpad = up(wl, 128)
    rowx, blk = pairs * CAP, nx * CAP
    prows = packed_rows(blk, feat)

    px = np.zeros((slots, slots), np.float32)
    for p in range(pairs):
        for s in range(nx):
            for c in range(CAP):
                px[p * blk + s * CAP + c, s * rowx + p * CAP + c] = 1
    pz = np.zeros((rows, rows), np.float32)
    for q in range(nz):
        for s in range(nx):
            for c in range(CAP):
                pz[(q % 2) * slots + (q // 2) * blk + s * CAP + c, (s * nz + q) * CAP + c] = 1
    slot = np.arange(slots)
    e_mat = (slot[:, None] // CAP == np.arange(experts)[None, :]).astype(np.float32)
    m_mat = np.broadcast_to((slot % CAP)[:, None], (slots, tok)).astype(np.float32)

    dma = pltpu.SemaphoreType.DMA
    vm = pltpu.VMEM
    groups = nh * ny
    scratch = [
        vm((slots, tok), BF16),
        vm((nx, rowx, fpad), BF16), vm((nx, rowx, fpad), BF16),
        vm((pairs, prows, 128), BF16), vm((2, pairs, prows, 128), BF16),
        vm((rows, feat), BF16), vm((2, pairs, prows, 128), BF16), vm((2, pairs, prows, 128), BF16),
        vm((2, pairs, prows, 128), BF16), vm((pairs, prows, 128), BF16),
        vm((nx, rowx, fpad), BF16), vm((nx, rowx, fpad), BF16),
        vm((groups, feat, tok), F32), vm((groups, feat, tok), BF16), vm((groups, feat, tok), BF16),
        vm((ny - 1, nh, feat, tok), BF16), vm((ny - 1, nh, feat, tok), BF16),
        vm((feat, tok), BF16), vm((feat, tok), BF16),
        vm((nx - 1, nz, hid, wpad), BF16), vm((nx - 1, nz, hid, wpad), BF16),
        vm((nz, hid, wpad), F32), vm((nz, hid, wpad), BF16), vm((nz, hid, wpad), BF16),
        pltpu.SemaphoreType.REGULAR((3,)),
        vm((hid, width), BF16), vm((rows, cols), BF16), vm((feat, cols), BF16),
        vm((rows, rows), BF16), dma((4,)),
    ]
    for count in (nx, nz, nz, nz, nz, nx, groups, ny, 1, nx, bits):
        scratch += [dma((count,)), dma((count,))]
    full = pl.BlockSpec(memory_space=pltpu.VMEM)
    hbm = pl.BlockSpec(memory_space=pl.ANY)
    in_t, dw_t, ew_out = pl.pallas_call(
        functools.partial(kernel, (nx, nz, ny, nh)),
        out_shape=(
            jax.ShapeDtypeStruct((feat, tok), BF16),
            jax.ShapeDtypeStruct((hid, wl), F32),
            jax.ShapeDtypeStruct((feat, cols), BF16),
        ),
        in_specs=[full] * 3 + [hbm] * 3 + [full, hbm, full, full],
        out_specs=(full, full, full),
        scratch_shapes=scratch,
        compiler_params=pltpu.CompilerParams(
            collective_id=0, has_side_effects=True, vmem_limit_bytes=56 * 1024 * 1024
        ),
    )(
        layer_input, routes.T, dense_cot.T, dense_weight.T, expert_cot, expert_weight,
        jnp.asarray(px, BF16), jnp.asarray(pz, BF16), jnp.asarray(e_mat, BF16),
        jnp.asarray(m_mat, F32),
    )
    return (in_t.T, dw_t.T, ew_out)


def solution(mesh, nx=NX, ny=NY):
    placed = (
        P("expert", None),
        P("expert", None),
        P("expert", ("dp", "tensor")),
        P(None, ("dp", "tensor")),
        P(None, "expert"),
        P(("dp", "tensor"), "expert"),
    )
    return jax.shard_map(
        functools.partial(body, nx, ny),
        mesh=mesh,
        in_specs=placed,
        out_specs=(
            P("expert", ("dp", "tensor")),
            P("expert", ("dp", "tensor")),
            P(("dp", "tensor"), "expert"),
        ),
        check_vma=False,
    )
```
